256 devices in a mesh: ctx: 16 (over x_hi, y, core), head: 16 (over z, x_lo).
Axes of the slice: x: 4 (x_hi: 2, x_lo: 2; x = x_hi * 2 + x_lo), y: 4, z: 8, core: 2. Of those that a mesh axis runs over, the one named last changes fastest.
Arguments:
- queries: bfloat16 [8192, 4096], P('ctx', 'head'), may hold values from -8 to 8
- keys: bfloat16 [8192, 1024], P('ctx', 'head'), may hold values from -4 to 4
- values: bfloat16 [8192, 1024], P('ctx', 'head'), may hold values from -6 to 6
- positions: int32 [8192], P('ctx'), may hold values from 0 to 8191, as said below
- out_weight: bfloat16 [4096, 4096], P('head'), may hold values from -0.125 to 0.125
Outputs:
- mixed_t: bfloat16 [4096, 8192], P('head', 'ctx')
The draws below stay inside these ranges and needn't reach their ends.
Inputs may be any that keep to these rules, and one draw needn't show every extreme that they name: A permutation of 0 to 8191; each aligned block of 256 rows holds 256 consecutive positions in rising order, starting at a multiple of 256.
All inputs are finite; a program needn't handle non-finite values.
Results may differ from the reference program's by a relative error of at most 0.024.
Values may be sent and summed in bfloat16 or wider, within the bound.
A program may use at most 64 MiB of HBM per device.

```python
import jax
import jax.numpy as jnp
from jax import lax

D = 4096
HD = 128
Q_HEADS = 32
KV_HEADS = 8
TOKENS = 8192
SPAN = 256
N_HEAD = 16


def draw_keys(key, part):
    key = jax.random.fold_in(key, 1)
    base = jnp.clip(jax.random.normal(key, (TOKENS, KV_HEADS, HD), jnp.float32), -4.0, 4.0)
    return base.reshape(TOKENS, KV_HEADS * HD).astype(jnp.bfloat16)


def draw_queries(key, part):
    key = jax.random.fold_in(key, 2)
    base = jnp.clip(jax.random.normal(key, (TOKENS, Q_HEADS, HD), jnp.float32), -4.0, 4.0)
    return base.reshape(TOKENS, Q_HEADS * HD).astype(jnp.bfloat16)


def draw_positions(key, part):
    key = jax.random.fold_in(key, 3)
    order = jax.random.permutation(key, TOKENS // SPAN)
    starts = order.astype(jnp.int32)[:, None] * SPAN
    return (starts + jnp.arange(SPAN, dtype=jnp.int32)[None, :]).reshape(TOKENS).astype(jnp.int32)


def strengthened(values, rng, source, target, shards_of, factor):
    def block_of(position):
        return (jnp.arange(values.shape[position]) // (values.shape[position] // shards_of)).reshape((-1,) + (1,) * (values.ndim - 1 - position))

    one_side = jax.random.permutation(rng, shards_of)[block_of(target)]
    second = (block_of(target) + shards_of // 2) % shards_of
    return jnp.where((block_of(source) == one_side) | (block_of(source) == second), factor * values, values)


def shard_levels(key, shape, pieces, least, largest):
    def one(axis_at, blocks):
        steps = jax.random.uniform(jax.random.fold_in(jax.random.fold_in(key, 6), axis_at), (blocks,), jnp.float32, least / len(pieces), largest / len(pieces))
        return jnp.repeat(jnp.exp(steps), shape[axis_at] // blocks).reshape((-1,) + (1,) * (len(shape) - axis_at - 1))

    loudness = one(*pieces[0])
    for cut in pieces[1:]:
        loudness = loudness * one(*cut)
    return loudness


def normal_values(key, extent, scale, reach, split=(), held_as=jnp.bfloat16):
    drawn = scale * jax.random.normal(key, extent, jnp.float32)
    if split:
        drawn = drawn * shard_levels(key, extent, split, -0.22, 0.18)
    return jnp.clip(drawn, -reach, reach).astype(held_as)


def bell_draw_with(own_key, shape, scale, most, shards, heavy, kind=jnp.bfloat16):
    values = scale * jax.random.normal(own_key, shape, jnp.float32)
    if shards:
        values = values * shard_levels(own_key, shape, shards, -0.22, 0.18)
    return jnp.clip(strengthened(values, jax.random.fold_in(own_key, 3), *heavy), -most, most).astype(kind)


def setup_inputs(seed: int = 0) -> dict:
    key_of = jax.random.split(jax.random.key(seed), 6)
    return {
        "queries": draw_queries(jax.random.fold_in(key_of[5], 71), 0),
        "keys": draw_keys(jax.random.fold_in(key_of[5], 71), 0),
        "values": normal_values(key_of[2], (TOKENS, KV_HEADS * HD), 1.0, 6.0, ((0, 16), (1, 16))),
        "positions": draw_positions(jax.random.fold_in(key_of[5], 71), 0),
        "out_weight": bell_draw_with(key_of[4], (Q_HEADS * HD, D), (Q_HEADS * HD) ** -0.5, 0.125, ((0, 16),), (0, 1, 16, 2.0)),
    }


SCALE = 0.08838834764831845


def reference(queries, keys, values, positions, out_weight):
    seq = queries.shape[0]
    group = Q_HEADS // KV_HEADS
    query_heads = queries.reshape(seq, Q_HEADS, HD).transpose(1, 0, 2)
    key_heads = jnp.repeat(keys.reshape(seq, KV_HEADS, HD).transpose(1, 0, 2), group, axis=0)
    value_heads = jnp.repeat(values.reshape(seq, KV_HEADS, HD).transpose(1, 0, 2), group, axis=0)
    visible = positions[None, :] <= positions[:, None]

    def one_head(operands):
        q_one, k_one, v_one = operands
        scores = jnp.dot(q_one, k_one.T, preferred_element_type=jnp.float32) * SCALE
        scores = jnp.where(visible, scores, jnp.float32(-1e30))
        top = jnp.max(scores, axis=1, keepdims=True)
        expo = jnp.where(visible, jnp.exp(scores - top), jnp.float32(0.0))
        total = jnp.sum(expo, axis=1, keepdims=True)
        summed = jnp.dot(expo.astype(jnp.bfloat16), v_one, preferred_element_type=jnp.float32)
        return (summed / total).astype(jnp.bfloat16)

    attended = lax.map(one_head, (query_heads, key_heads, value_heads))
    attended = attended.transpose(1, 0, 2).reshape(seq, Q_HEADS * HD)
    width = Q_HEADS * HD // N_HEAD
    weight_groups = out_weight.reshape(N_HEAD, width, D)
    attended_groups = attended.reshape(seq, N_HEAD, width).transpose(1, 0, 2)

    def add_group(carry, pair):
        w_group, a_group = pair
        partial_sum = lax.dot_general(w_group, a_group, (((0,), (1,)), ((), ())), preferred_element_type=jnp.float32)
        rounded = lax.optimization_barrier(partial_sum.astype(jnp.bfloat16))
        return carry + rounded.astype(jnp.float32), None

    mixed, unused = lax.scan(add_group, jnp.zeros((D, seq), jnp.float32), (weight_groups, attended_groups))
    return mixed.astype(jnp.bfloat16)
```

```python
import functools

import jax
import jax.numpy as jnp
from jax import lax
from jax.experimental import pallas as pl
from jax.experimental.pallas import tpu as pltpu
from jax.sharding import PartitionSpec as P

SCALE = 0.08838834764831845
LOG2E = 1.4426950408889634
C = SCALE * LOG2E
NEG = -1e30
HIDE = 1e30
ROWS = 512
SPAN = 256
PARTS = 4
PART = ROWS // PARTS
OFFSETS = (4, 3, -3, 2, -2, 1, -1, 0)
f32 = jnp.float32
bf16 = jnp.bfloat16
MESH = pl.DeviceIdType.MESH


def kernel(
    q_ref, k_ref, v_ref, pos_ref, w_hbm, out_ref,
    kv, posb, qT, scores, top, shift, total, acc, w_own, wT, w_oth, a_own, a_oth,
    z_out, z_in, z_out4, z_in4,
    load_sem, kv_send, kv_recv, kv_cross, pos_send, pos_recv, w_send, w_recv, w_cross,
    a_send, a_recv, z_send, z_recv,
):
    ctx = lax.axis_index("ctx")
    head = lax.axis_index("head")
    core = lax.rem(ctx, 2)
    y = lax.rem(lax.div(ctx, 2), 4)
    xh = lax.div(ctx, 8)
    z = lax.div(head, 2)
    xl = lax.rem(head, 2)
    x = xh * 2 + xl

    def device(dx, dy, dz, dcore):
        nx = lax.rem(x + dx + 4, 4)
        ny = lax.rem(y + dy + 4, 4)
        nz = lax.rem(z + dz + 8, 8)
        nc = lax.rem(core + dcore, 2)
        return {"ctx": (lax.div(nx, 2) * 4 + ny) * 2 + nc, "head": nz * 2 + lax.rem(nx, 2)}

    def first(d):
        return device(core * d, (1 - core) * d, 0, 0)

    def second(d):
        return device((1 - core) * d, core * d, 0, 0)

    other_core = device(0, 0, 0, 1)
    mate = device(1 - 2 * xl, 0, 0, 0)

    def piece_of(f, s, lane):
        own = core if lane == 0 else 1 - core
        px = lax.rem(x + own * f + (1 - own) * s, 4)
        py = lax.rem(y + (1 - own) * f + own * s, 4)
        return (lax.div(px, 2) * 4 + py) * 2 + own, lax.rem(px, 2)

    def block_of(other_hi, dy, lane):
        own = core if lane == 0 else 1 - core
        bh = 1 - xh if other_hi else xh
        return (bh * 4 + lax.rem(y + dy + 4, 4)) * 2 + own

    def remote(src, dst, send_sem, recv_sem, target):
        return pltpu.make_async_remote_copy(
            src_ref=src, dst_ref=dst, send_sem=send_sem, recv_sem=recv_sem,
            device_id=target, device_id_type=MESH,
        )

    started = []

    def send(src, dst, send_sem, recv_sem, target):
        copy = remote(src, dst, send_sem, recv_sem, target)
        copy.start()
        started.append(copy)

    def arrived(dst, recv_sem):
        remote(dst, dst, load_sem.at[0], recv_sem, other_core).wait_recv()

    load = pltpu.make_async_copy(w_hbm, w_own, load_sem.at[0])
    load.start()

    barrier = pltpu.get_barrier_semaphore()
    relations = [
        (h, dy, c) for h in range(2) for dy in range(4) for c in range(2) if (h, dy, c) != (0, 0, 0)
    ]
    friends = [device(2 * h, dy, 0, c) for h, dy, c in relations]
    friends += [device(1, 0, 0, 0), device(-1, 0, 0, 0), device(0, 0, 1, 0), device(0, 0, -1, 0)]
    for friend in friends:
        pl.semaphore_signal(barrier, inc=1, device_id=friend, device_id_type=MESH)

    my_block = block_of(False, 0, 0)
    kv[my_block, xl, 0:64, :] = k_ref[...]
    kv[my_block, xl, 64:128, :] = v_ref[...]
    lane = lax.broadcasted_iota(jnp.int32, (1, 128), 1)
    posb[my_block, :, 0:128] = pos_ref[:, 0:128] - lane
    posb[my_block, :, 128:256] = pos_ref[:, SPAN : SPAN + 128] - lane
    pl.semaphore_wait(barrier, len(friends))

    sent = [0]

    def pass_on(f, s, target, f_there, s_there, half=None):
        block, side = piece_of(f, s, 0)
        view = kv.at[block, side] if half is None else kv.at[block, side, pl.ds(64 * half, 64)]
        send(view, view, kv_send.at[sent[0]],
             kv_recv.at[f_there % 4, s_there % 4, 0 if half is None else half], target)
        sent[0] += 1

    def cross(f, s):
        block, side = piece_of(f, s, 0)
        view = kv.at[block, side]
        send(view, view, kv_send.at[sent[0]], kv_cross.at[f, s], other_core)
        sent[0] += 1

    def to_second(f):
        pass_on(f, 0, second(1), f, -1)
        pass_on(f, 0, second(-1), f, 1)

    def wait_piece(f, s):
        block, side = piece_of(f, s, 0)
        if f == 2 or s == 2:
            for half in range(2):
                if f == 2 and s != 0 and s != 2:
                    continue
                arrived(kv.at[block, side, pl.ds(64 * half, 64)], kv_recv.at[f, s, half])
            if f == 2 and s != 0 and s != 2:
                arrived(kv.at[block, side], kv_recv.at[f, s, 0])
        else:
            arrived(kv.at[block, side], kv_recv.at[f, s, 0])
        if s == 0:
            if f == 3:
                to_second(f)
                pass_on(f, 0, first(1), 2, 0, half=0)
            elif f == 1:
                to_second(f)
                pass_on(f, 0, first(-1), 2, 0, half=1)
            elif f == 2:
                to_second(f)
        elif s == 3:
            pass_on(f, s, second(1), f, 2, half=0)
        elif s == 1:
            pass_on(f, s, second(-1), f, 2, half=1)
        cross(f, s)

    def wait_cross(f, s):
        block, side = piece_of(f, s, 1)
        arrived(kv.at[block, side], kv_cross.at[f, s])

    pass_on(0, 0, first(1), -1, 0)
    pass_on(0, 0, first(-1), 1, 0)
    to_second(0)
    cross(0, 0)
    for i, (h, dy, c) in enumerate(relations):
        there = relations.index((h, (4 - dy) % 4, c))
        send(posb.at[my_block], posb.at[my_block], pos_send.at[i], pos_recv.at[there],
             device(2 * h, dy, 0, c))

    for h in range(2):
        t = q_ref[:, h * 128 : (h + 1) * 128].T
        gap = jnp.zeros((64, ROWS), bf16)
        qT[h] = jnp.concatenate([t[:64], gap, t[64:], gap], axis=0)
    top[...] = jnp.full(top.shape, NEG, f32)
    total[...] = jnp.zeros(total.shape, f32)
    acc[...] = jnp.zeros(acc.shape, f32)
    load.wait()
    for tile in range(16):
        wT[tile] = w_own[:, tile * 256 : (tile + 1) * 256].T

    row_pos = pos_ref[...]

    def stage_a(n, block, own):
        par = n % 2
        k = jnp.concatenate([kv[block, 0], kv[block, 1]], axis=0).T
        starts = [
            jnp.concatenate([posb[block, :, j * 128 : (j + 1) * 128]] * 4, axis=1) for j in range(2)
        ]
        seen = [start <= row_pos for start in starts]
        if own:
            inside = lax.broadcasted_iota(jnp.int32, (SPAN, ROWS), 0)
            masks = [inside + start <= row_pos for start in starts]
        for h in range(2):
            s = jnp.dot(k, qT[h], preferred_element_type=f32)
            if own:
                s = jnp.concatenate(
                    [jnp.where(masks[j], s[j * SPAN : (j + 1) * SPAN], NEG) for j in range(2)], axis=0
                )
            scores[par, h] = s
            new = top[par, h]
            for j in range(2):
                most = jnp.max(s[j * SPAN : (j + 1) * SPAN], axis=0, keepdims=True)
                new = jnp.maximum(new, jnp.where(seen[j], most, NEG))
            top[1 - par, h] = new
            for j in range(2):
                shift[par, h, j] = new * C + jnp.where(seen[j], 0.0, HIDE)

    def stage_b(n, block):
        par = n % 2
        v = jnp.concatenate([kv[block, 0, 64:], kv[block, 1, 64:]], axis=0)
        for h in range(2):
            fade = jnp.exp2((top[par, h] - top[1 - par, h]) * C)
            expo = [
                jnp.exp2(scores[par, h, j * SPAN : (j + 1) * SPAN] * C - shift[par, h, j])
                for j in range(2)
            ]
            total[h] = total[h] * fade + (
                jnp.sum(expo[0], axis=0, keepdims=True) + jnp.sum(expo[1], axis=0, keepdims=True)
            )
            weights = jnp.concatenate(expo, axis=0).astype(bf16)
            acc[h] = acc[h] * fade + jnp.dot(v, weights, preferred_element_type=f32)

    done = []

    def absorb(other_hi, dy, which):
        n = len(done)
        block = block_of(other_hi, dy, which)
        own = n == 0
        if own:
            stage_a(n, block, True)
        else:
            stage_b_then_a(n, block)
        done.append(block)

    def stage_b_then_a(n, block):
        par = (n - 1) % 2
        for h in range(2):
            fades[h] = jnp.exp2((top[par, h] - top[1 - par, h]) * C)
        stage_a(n, block, False)
        stage_b_with(n - 1, done[n - 1])

    fades = [None, None]

    def stage_b_with(n, block):
        par = n % 2
        v = jnp.concatenate([kv[block, 0, 64:], kv[block, 1, 64:]], axis=0)
        for h in range(2):
            fade = fades[h]
            expo = [
                jnp.exp2(scores[par, h, j * SPAN : (j + 1) * SPAN] * C - shift[par, h, j])
                for j in range(2)
            ]
            total[h] = total[h] * fade + (
                jnp.sum(expo[0], axis=0, keepdims=True) + jnp.sum(expo[1], axis=0, keepdims=True)
            )
            weights = jnp.concatenate(expo, axis=0).astype(bf16)
            acc[h] = acc[h] * fade + jnp.dot(v, weights, preferred_element_type=f32)

    for f, s in ((1, 0), (3, 0), (0, 1), (0, 3)):
        wait_piece(f, s)
    absorb(False, 0, 0)
    for i, (h, dy, c) in enumerate(relations):
        block = (lax.rem(xh + h, 2) * 4 + lax.rem(y + dy, 4)) * 2 + lax.rem(core + c, 2)
        arrived(posb.at[block], pos_recv.at[i])
    wait_cross(0, 0)
    for f, s in ((1, 0), (3, 0), (0, 1), (0, 3)):
        wait_cross(f, s)
    absorb(False, 0, 1)
    for f, s in ((1, 1), (1, 3), (3, 1), (3, 3)):
        wait_piece(f, s)
    absorb(False, 1, 0)
    absorb(False, -1, 0)
    for f, s in ((2, 0), (0, 2)):
        wait_piece(f, s)
    absorb(True, 0, 0)
    for f, s in ((1, 1), (1, 3), (3, 1), (3, 3)):
        wait_cross(f, s)
    absorb(False, 1, 1)
    absorb(False, -1, 1)
    for f, s in ((2, 1), (2, 3), (1, 2), (3, 2)):
        wait_piece(f, s)
    for f, s in ((2, 0), (0, 2)):
        wait_cross(f, s)
    absorb(True, 0, 1)
    absorb(False, 2, 0)
    for j in range(2):
        for side, d in ((0, 1), (1, -1)):
            slot = 4 * j + 2 * side + core
            offset = sum(
                (jnp.where(slot == i, o, 0) for i, o in enumerate(OFFSETS)), jnp.int32(0)
            )
            tile = lax.rem(z + offset + 8, 8) * 2 + 1 - xl
            send(wT.at[tile], w_oth.at[slot], w_send.at[j, side, 0], w_recv.at[j, side],
                 device(d, 0, 0, 0))
    absorb(True, 1, 0)
    absorb(True, -1, 0)
    wait_piece(2, 2)
    for f, s in ((2, 1), (2, 3), (1, 2), (3, 2)):
        wait_cross(f, s)
    absorb(False, 2, 1)
    absorb(True, 1, 1)
    absorb(True, -1, 1)
    absorb(True, 2, 0)
    wait_cross(2, 2)
    absorb(True, 2, 1)
    last = len(done) - 1
    stage_b(last, done[last])

    for t in range(PARTS):
        cols = slice(t * PART, (t + 1) * PART)
        for h in range(2):
            a_own[t, h * 128 : (h + 1) * 128, :] = (acc[h, :, cols] / total[h, :, cols]).astype(bf16)
        send(a_own.at[t], a_oth.at[t], a_send.at[t], a_recv.at[t], mate)

    def weights_in(j):
        for side in range(2):
            slot = 4 * j + 2 * side + core
            arrived(w_oth.at[slot], w_recv.at[j, side])
            send(w_oth.at[slot], w_oth.at[slot], w_send.at[j, side, 1], w_cross.at[j, side], other_core)

    def weights_crossed(j):
        for side in range(2):
            arrived(w_oth.at[4 * j + 2 * side + 1 - core], w_cross.at[j, side])

    weights_in(0)
    weights_in(1)
    weights_crossed(0)

    def project(offset, t):
        tile = lax.rem(z + offset + 8, 8) * 2 + xl
        return jnp.dot(wT[tile], a_own[t], preferred_element_type=f32) + jnp.dot(
            w_oth[OFFSETS.index(offset)], a_oth[t], preferred_element_type=f32
        )

    for t in range(PARTS):
        arrived(a_oth.at[t], a_recv.at[t])
        part = project(4, t)
        for d, sign in ((0, 1), (1, -1)):
            z_out4[d, t] = part[d * 128 : (d + 1) * 128].astype(bf16)
            send(z_out4.at[d, t], z_in4.at[d, t], z_send.at[d, 3, t], z_recv.at[d, 3, t],
                 device(0, 0, sign, 0))
    weights_crossed(1)
    for k in (3, 2, 1):
        for t in range(PARTS):
            for d, sign in ((0, 1), (1, -1)):
                part = project(sign * k, t)
                if k == 3:
                    arrived(z_in4.at[d, t], z_recv.at[d, 3, t])
                    more = part[d * 128 : (d + 1) * 128] + z_in4[d, t].astype(f32)
                    rest = part[(1 - d) * 128 : (2 - d) * 128]
                    z_out[d, k - 1, t, d * 128 : (d + 1) * 128, :] = more.astype(bf16)
                    z_out[d, k - 1, t, (1 - d) * 128 : (2 - d) * 128, :] = rest.astype(bf16)
                else:
                    arrived(z_in.at[d, k, t], z_recv.at[d, k, t])
                    z_out[d, k - 1, t] = (part + z_in[d, k, t].astype(f32)).astype(bf16)
                send(z_out.at[d, k - 1, t], z_in.at[d, k - 1, t], z_send.at[d, k - 1, t],
                     z_recv.at[d, k - 1, t], device(0, 0, sign, 0))
    for t in range(PARTS):
        part = project(0, t)
        for d in range(2):
            arrived(z_in.at[d, 0, t], z_recv.at[d, 0, t])
        out_ref[:, t * PART : (t + 1) * PART] = (
            part + (z_in[0, 0, t].astype(f32) + z_in[1, 0, t].astype(f32))
        ).astype(bf16)
    for copy in started:
        copy.wait_send()


def body(queries, keys, values, positions, out_weight):
    vmem = pl.BlockSpec(memory_space=pltpu.VMEM)
    dma = pltpu.SemaphoreType.DMA
    return pl.pallas_call(
        kernel,
        out_shape=jax.ShapeDtypeStruct((256, ROWS), bf16),
        in_specs=[vmem, vmem, vmem, vmem, pl.BlockSpec(memory_space=pl.ANY)],
        out_specs=vmem,
        scratch_shapes=[
            pltpu.VMEM((16, 2, 128, ROWS), bf16),
            pltpu.VMEM((16, 1, 256), jnp.int32),
            pltpu.VMEM((2, 256, ROWS), bf16),
            pltpu.VMEM((2, 2, ROWS, ROWS), f32),
            pltpu.VMEM((2, 2, 1, ROWS), f32),
            pltpu.VMEM((2, 2, 2, 1, ROWS), f32),
            pltpu.VMEM((2, 1, ROWS), f32),
            pltpu.VMEM((2, 128, ROWS), f32),
            pltpu.VMEM((256, 4096), bf16),
            pltpu.VMEM((16, 256, 256), bf16),
            pltpu.VMEM((8, 256, 256), bf16),
            pltpu.VMEM((PARTS, 256, PART), bf16),
            pltpu.VMEM((PARTS, 256, PART), bf16),
            pltpu.VMEM((2, 3, PARTS, 256, PART), bf16),
            pltpu.VMEM((2, 3, PARTS, 256, PART), bf16),
            pltpu.VMEM((2, PARTS, 128, PART), bf16),
            pltpu.VMEM((2, PARTS, 128, PART), bf16),
            dma((1,)),
            dma((36,)),
            dma((4, 4, 2)),
            dma((4, 4)),
            dma((15,)),
            dma((15,)),
            dma((2, 2, 2)),
            dma((2, 2)),
            dma((2, 2)),
            dma((PARTS,)),
            dma((PARTS,)),
            dma((2, 4, PARTS)),
            dma((2, 4, PARTS)),
        ],
        compiler_params=pltpu.CompilerParams(
            collective_id=0, has_side_effects=True, vmem_limit_bytes=48 << 20
        ),
        cost_estimate=pl.CostEstimate(flops=6_000_000_000, bytes_accessed=4_000_000, transcendentals=8_400_000),
    )(queries, keys.T, values.T, positions.reshape(1, ROWS), out_weight)


def solution(mesh):
    in_specs = (P("ctx", "head"), P("ctx", "head"), P("ctx", "head"), P("ctx"), P("head", None))
    out_specs = P("head", "ctx")
    return jax.shard_map(body, mesh=mesh, in_specs=in_specs, out_specs=out_specs, check_vma=False)
```

```python
import functools

import jax
import jax.numpy as jnp
from jax import lax
from jax.experimental import pallas as pl
from jax.experimental.pallas import tpu as pltpu
from jax.sharding import PartitionSpec as P

SCALE = 0.08838834764831845
LOG2E = 1.4426950408889634
C = SCALE * LOG2E
NEG = -1e30
HIDE = 1e30
ROWS = 512
SPAN = 256
PARTS = 4
PART = ROWS // PARTS
OFFSETS = (4, 3, -3, 2, -2, 1, -1, 0)
f32 = jnp.float32
bf16 = jnp.bfloat16
MESH = pl.DeviceIdType.MESH


def kernel(
    q_hbm, k_hbm, v_hbm, pos_hbm, w_hbm, out_ref,
    q_ref, pos_ref, out_v, kv, posb, qT, scores, top, shift, total, acc, w_own, wT, w_oth, a_own, a_oth,
    z_out, z_in, z_out4, z_in4,
    load_sem, kv_send, kv_recv, kv_cross, pos_send, pos_recv, w_send, w_recv, w_cross,
    a_send, a_recv, z_send, z_recv,
):
    ctx = lax.axis_index("ctx")
    head = lax.axis_index("head")
    core = lax.rem(ctx, 2)
    y = lax.rem(lax.div(ctx, 2), 4)
    xh = lax.div(ctx, 8)
    z = lax.div(head, 2)
    xl = lax.rem(head, 2)
    x = xh * 2 + xl

    def device(dx, dy, dz, dcore):
        nx = lax.rem(x + dx + 4, 4)
        ny = lax.rem(y + dy + 4, 4)
        nz = lax.rem(z + dz + 8, 8)
        nc = lax.rem(core + dcore, 2)
        return {"ctx": (lax.div(nx, 2) * 4 + ny) * 2 + nc, "head": nz * 2 + lax.rem(nx, 2)}

    def first(d):
        return device(core * d, (1 - core) * d, 0, 0)

    def second(d):
        return device((1 - core) * d, core * d, 0, 0)

    other_core = device(0, 0, 0, 1)
    mate = device(1 - 2 * xl, 0, 0, 0)

    def piece_of(f, s, lane):
        own = core if lane == 0 else 1 - core
        px = lax.rem(x + own * f + (1 - own) * s, 4)
        py = lax.rem(y + (1 - own) * f + own * s, 4)
        return (lax.div(px, 2) * 4 + py) * 2 + own, lax.rem(px, 2)

    def block_of(other_hi, dy, lane):
        own = core if lane == 0 else 1 - core
        bh = 1 - xh if other_hi else xh
        return (bh * 4 + lax.rem(y + dy + 4, 4)) * 2 + own

    def remote(src, dst, send_sem, recv_sem, target):
        return pltpu.make_async_remote_copy(
            src_ref=src, dst_ref=dst, send_sem=send_sem, recv_sem=recv_sem,
            device_id=target, device_id_type=MESH,
        )

    started = []

    def send(src, dst, send_sem, recv_sem, target):
        copy = remote(src, dst, send_sem, recv_sem, target)
        copy.start()
        started.append(copy)

    def arrived(dst, recv_sem):
        remote(dst, dst, load_sem.at[0], recv_sem, other_core).wait_recv()

    loads = []

    def load(src, dst):
        copy = pltpu.make_async_copy(src, dst, load_sem.at[len(loads)])
        copy.start()
        loads.append(copy)

    my_block = block_of(False, 0, 0)
    load(k_hbm, kv.at[my_block, xl, pl.ds(0, 64)])
    load(v_hbm, kv.at[my_block, xl, pl.ds(64, 64)])
    load(pos_hbm, pos_ref)
    load(q_hbm, q_ref)
    load(w_hbm, w_own)

    barrier = pltpu.get_barrier_semaphore()
    relations = [
        (h, dy, c) for h in range(2) for dy in range(4) for c in range(2) if (h, dy, c) != (0, 0, 0)
    ]
    friends = [device(2 * h, dy, 0, c) for h, dy, c in relations]
    friends += [device(1, 0, 0, 0), device(-1, 0, 0, 0), device(0, 0, 1, 0), device(0, 0, -1, 0)]
    for friend in friends:
        pl.semaphore_signal(barrier, inc=1, device_id=friend, device_id_type=MESH)
    for i in range(3):
        loads[i].wait()
    lane = lax.broadcasted_iota(jnp.int32, (1, 128), 1)
    posb[my_block, :, 0:128] = pos_ref[:, 0:128] - lane
    posb[my_block, :, 128:256] = pos_ref[:, SPAN : SPAN + 128] - lane
    pl.semaphore_wait(barrier, len(friends))

    sent = [0]

    def pass_on(f, s, target, f_there, s_there, half=None):
        block, side = piece_of(f, s, 0)
        view = kv.at[block, side] if half is None else kv.at[block, side, pl.ds(64 * half, 64)]
        send(view, view, kv_send.at[sent[0]],
             kv_recv.at[f_there % 4, s_there % 4, 0 if half is None else half], target)
        sent[0] += 1

    def cross(f, s):
        block, side = piece_of(f, s, 0)
        view = kv.at[block, side]
        send(view, view, kv_send.at[sent[0]], kv_cross.at[f, s], other_core)
        sent[0] += 1

    def to_second(f):
        pass_on(f, 0, second(1), f, -1)
        pass_on(f, 0, second(-1), f, 1)

    def wait_piece(f, s):
        block, side = piece_of(f, s, 0)
        if s == 2 or (f, s) == (2, 0):
            for half in range(2):
                arrived(kv.at[block, side, pl.ds(64 * half, 64)], kv_recv.at[f, s, half])
        else:
            arrived(kv.at[block, side], kv_recv.at[f, s, 0])
        if s == 0:
            to_second(f)
        elif s == 3:
            pass_on(f, s, second(1), f, 2, half=0)
        elif s == 1:
            pass_on(f, s, second(-1), f, 2, half=1)
        cross(f, s)

    def wait_cross(f, s):
        block, side = piece_of(f, s, 1)
        arrived(kv.at[block, side], kv_cross.at[f, s])

    pass_on(0, 0, first(1), -1, 0)
    pass_on(0, 0, first(-1), 1, 0)
    pass_on(0, 0, first(2), 2, 0, half=0)
    pass_on(0, 0, first(-2), 2, 0, half=1)
    to_second(0)
    cross(0, 0)
    for i, (h, dy, c) in enumerate(relations):
        there = relations.index((h, (4 - dy) % 4, c))
        send(posb.at[my_block], posb.at[my_block], pos_send.at[i], pos_recv.at[there],
             device(2 * h, dy, 0, c))

    def weights_out(j):
        for side, d in ((0, 1), (1, -1)):
            slot = 4 * j + 2 * side + core
            offset = sum(
                (jnp.where(slot == i, o, 0) for i, o in enumerate(OFFSETS)), jnp.int32(0)
            )
            tile = lax.rem(z + offset + 8, 8) * 2 + 1 - xl
            send(wT.at[tile], w_oth.at[slot], w_send.at[j, side, 0], w_recv.at[j, side],
                 device(d, 0, 0, 0))

    def weights_in(j):
        for side in range(2):
            slot = 4 * j + 2 * side + core
            arrived(w_oth.at[slot], w_recv.at[j, side])
            send(w_oth.at[slot], w_oth.at[slot], w_send.at[j, side, 1], w_cross.at[j, side], other_core)

    def weights_crossed(j):
        for side in range(2):
            arrived(w_oth.at[4 * j + 2 * side + 1 - core], w_cross.at[j, side])

    loads[4].wait()
    for tile in range(16):
        wT[tile] = w_own[:, tile * 256 : (tile + 1) * 256].T
    weights_out(0)
    loads[3].wait()
    for h in range(2):
        t = q_ref[:, h * 128 : (h + 1) * 128].T
        gap = jnp.zeros((64, ROWS), bf16)
        qT[h] = jnp.concatenate([t[:64], gap, t[64:], gap], axis=0)
    top[...] = jnp.full(top.shape, NEG, f32)
    total[...] = jnp.zeros(total.shape, f32)
    acc[...] = jnp.zeros(acc.shape, f32)

    row_pos = pos_ref[...]

    def stage_a(n, block, own):
        par = n % 2
        k = jnp.concatenate([kv[block, 0], kv[block, 1]], axis=0).T
        starts = [
            jnp.concatenate([posb[block, :, j * 128 : (j + 1) * 128]] * 4, axis=1) for j in range(2)
        ]
        seen = [start <= row_pos for start in starts]
        if own:
            inside = lax.broadcasted_iota(jnp.int32, (SPAN, ROWS), 0)
            masks = [inside + start <= row_pos for start in starts]
        for h in range(2):
            s = jnp.dot(k, qT[h], preferred_element_type=f32)
            if own:
                s = jnp.concatenate(
                    [jnp.where(masks[j], s[j * SPAN : (j + 1) * SPAN], NEG) for j in range(2)], axis=0
                )
            scores[par, h] = s
            new = top[par, h]
            for j in range(2):
                most = jnp.max(s[j * SPAN : (j + 1) * SPAN], axis=0, keepdims=True)
                new = jnp.maximum(new, jnp.where(seen[j], most, NEG))
            top[1 - par, h] = new
            for j in range(2):
                shift[par, h, j] = new * C + jnp.where(seen[j], 0.0, HIDE)

    def stage_b(n, block):
        par = n % 2
        v = jnp.concatenate([kv[block, 0, 64:], kv[block, 1, 64:]], axis=0)
        for h in range(2):
            fade = jnp.exp2((top[par, h] - top[1 - par, h]) * C)
            expo = [
                jnp.exp2(scores[par, h, j * SPAN : (j + 1) * SPAN] * C - shift[par, h, j])
                for j in range(2)
            ]
            total[h] = total[h] * fade + (
                jnp.sum(expo[0], axis=0, keepdims=True) + jnp.sum(expo[1], axis=0, keepdims=True)
            )
            weights = jnp.concatenate(expo, axis=0).astype(bf16)
            acc[h] = acc[h] * fade + jnp.dot(v, weights, preferred_element_type=f32)

    done = []

    def absorb(other_hi, dy, which):
        n = len(done)
        block = block_of(other_hi, dy, which)
        own = n == 0
        if own:
            stage_a(n, block, True)
        else:
            stage_b_then_a(n, block)
        done.append(block)

    def stage_b_then_a(n, block):
        par = (n - 1) % 2
        for h in range(2):
            fades[h] = jnp.exp2((top[par, h] - top[1 - par, h]) * C)
        stage_a(n, block, False)
        stage_b_with(n - 1, done[n - 1])

    fades = [None, None]

    def stage_b_with(n, block):
        par = n % 2
        v = jnp.concatenate([kv[block, 0, 64:], kv[block, 1, 64:]], axis=0)
        for h in range(2):
            fade = fades[h]
            expo = [
                jnp.exp2(scores[par, h, j * SPAN : (j + 1) * SPAN] * C - shift[par, h, j])
                for j in range(2)
            ]
            total[h] = total[h] * fade + (
                jnp.sum(expo[0], axis=0, keepdims=True) + jnp.sum(expo[1], axis=0, keepdims=True)
            )
            weights = jnp.concatenate(expo, axis=0).astype(bf16)
            acc[h] = acc[h] * fade + jnp.dot(v, weights, preferred_element_type=f32)

    for f, s in ((1, 0), (3, 0), (2, 0), (0, 1), (0, 3)):
        wait_piece(f, s)
    absorb(False, 0, 0)
    for i, (h, dy, c) in enumerate(relations):
        block = (lax.rem(xh + h, 2) * 4 + lax.rem(y + dy, 4)) * 2 + lax.rem(core + c, 2)
        arrived(posb.at[block], pos_recv.at[i])
    for f, s in ((0, 0), (1, 0), (3, 0), (0, 1), (0, 3)):
        wait_cross(f, s)
    absorb(False, 0, 1)
    for f, s in ((0, 2), (1, 1), (1, 3)):
        wait_piece(f, s)
    absorb(True, 0, 0)
    for f, s in ((3, 1), (3, 3)):
        wait_piece(f, s)
    absorb(False, 1, 0)
    weights_in(0)
    absorb(False, -1, 0)
    for f, s in ((2, 1), (2, 3)):
        wait_piece(f, s)
    for f, s in ((2, 0), (0, 2)):
        wait_cross(f, s)
    absorb(True, 0, 1)
    for f, s in ((1, 1), (1, 3), (3, 1), (3, 3)):
        wait_cross(f, s)
    absorb(False, 1, 1)
    for f, s in ((1, 2), (3, 2)):
        wait_piece(f, s)
    absorb(False, -1, 1)
    absorb(False, 2, 0)
    wait_piece(2, 2)
    absorb(True, 1, 0)
    absorb(True, -1, 0)
    for f, s in ((2, 1), (2, 3), (1, 2), (3, 2)):
        wait_cross(f, s)
    absorb(False, 2, 1)
    absorb(True, 1, 1)
    absorb(True, -1, 1)
    weights_crossed(0)
    absorb(True, 2, 0)
    wait_cross(2, 2)
    absorb(True, 2, 1)
    last = len(done) - 1
    stage_b(last, done[last])

    for t in range(PARTS):
        cols = slice(t * PART, (t + 1) * PART)
        for h in range(2):
            scale = 1.0 / total[h, :, cols]
            a_own[t, h * 128 : (h + 1) * 128, :] = (acc[h, :, cols] * scale).astype(bf16)
        send(a_own.at[t], a_oth.at[t], a_send.at[t], a_recv.at[t], mate)

    def project(offset, t):
        tile = lax.rem(z + offset + 8, 8) * 2 + xl
        return jnp.dot(wT[tile], a_own[t], preferred_element_type=f32) + jnp.dot(
            w_oth[OFFSETS.index(offset)], a_oth[t], preferred_element_type=f32
        )

    for t in range(PARTS):
        arrived(a_oth.at[t], a_recv.at[t])
        part = project(4, t)
        for d, sign in ((0, 1), (1, -1)):
            z_out4[d, t] = part[d * 128 : (d + 1) * 128].astype(bf16)
            send(z_out4.at[d, t], z_in4.at[d, t], z_send.at[d, 3, t], z_recv.at[d, 3, t],
                 device(0, 0, sign, 0))
    weights_out(1)
    for k in (3, 2, 1):
        if k == 2:
            weights_in(1)
            weights_crossed(1)
        for t in range(PARTS):
            for d, sign in ((0, 1), (1, -1)):
                part = project(sign * k, t)
                if k == 3:
                    arrived(z_in4.at[d, t], z_recv.at[d, 3, t])
                    more = part[d * 128 : (d + 1) * 128] + z_in4[d, t].astype(f32)
                    rest = part[(1 - d) * 128 : (2 - d) * 128]
                    z_out[d, k - 1, t, d * 128 : (d + 1) * 128, :] = more.astype(bf16)
                    z_out[d, k - 1, t, (1 - d) * 128 : (2 - d) * 128, :] = rest.astype(bf16)
                else:
                    arrived(z_in.at[d, k, t], z_recv.at[d, k, t])
                    z_out[d, k - 1, t] = (part + z_in[d, k, t].astype(f32)).astype(bf16)
                send(z_out.at[d, k - 1, t], z_in.at[d, k - 1, t], z_send.at[d, k - 1, t],
                     z_recv.at[d, k - 1, t], device(0, 0, sign, 0))
    for t in range(PARTS):
        part = project(0, t)
        for d in range(2):
            arrived(z_in.at[d, 0, t], z_recv.at[d, 0, t])
        cols = pl.ds(t * PART, PART)
        out_v[:, cols] = (part + (z_in[0, 0, t].astype(f32) + z_in[1, 0, t].astype(f32))).astype(bf16)
        load(out_v.at[:, cols], out_ref.at[:, cols])
    for copy in loads[5:]:
        copy.wait()
    for copy in started:
        copy.wait_send()


def body(queries, keys, values, positions, out_weight):
    hbm = pl.BlockSpec(memory_space=pltpu.HBM)
    dma = pltpu.SemaphoreType.DMA
    return pl.pallas_call(
        kernel,
        out_shape=jax.ShapeDtypeStruct((256, ROWS), bf16),
        in_specs=[hbm] * 5,
        out_specs=hbm,
        scratch_shapes=[
            pltpu.VMEM((ROWS, 256), bf16),
            pltpu.VMEM((1, ROWS), jnp.int32),
            pltpu.VMEM((256, ROWS), bf16),
            pltpu.VMEM((16, 2, 128, ROWS), bf16),
            pltpu.VMEM((16, 1, 256), jnp.int32),
            pltpu.VMEM((2, 256, ROWS), bf16),
            pltpu.VMEM((2, 2, ROWS, ROWS), f32),
            pltpu.VMEM((2, 2, 1, ROWS), f32),
            pltpu.VMEM((2, 2, 2, 1, ROWS), f32),
            pltpu.VMEM((2, 1, ROWS), f32),
            pltpu.VMEM((2, 128, ROWS), f32),
            pltpu.VMEM((256, 4096), bf16),
            pltpu.VMEM((16, 256, 256), bf16),
            pltpu.VMEM((8, 256, 256), bf16),
            pltpu.VMEM((PARTS, 256, PART), bf16),
            pltpu.VMEM((PARTS, 256, PART), bf16),
            pltpu.VMEM((2, 3, PARTS, 256, PART), bf16),
            pltpu.VMEM((2, 3, PARTS, 256, PART), bf16),
            pltpu.VMEM((2, PARTS, 128, PART), bf16),
            pltpu.VMEM((2, PARTS, 128, PART), bf16),
            dma((5 + PARTS,)),
            dma((36,)),
            dma((4, 4, 2)),
            dma((4, 4)),
            dma((15,)),
            dma((15,)),
            dma((2, 2, 2)),
            dma((2, 2)),
            dma((2, 2)),
            dma((PARTS,)),
            dma((PARTS,)),
            dma((2, 4, PARTS)),
            dma((2, 4, PARTS)),
        ],
        compiler_params=pltpu.CompilerParams(
            collective_id=0, has_side_effects=True, vmem_limit_bytes=56 << 20
        ),
        cost_estimate=pl.CostEstimate(flops=6_000_000_000, bytes_accessed=4_000_000, transcendentals=8_400_000),
    )(queries, keys.T, values.T, positions.reshape(1, ROWS), out_weight)


def solution(mesh):
    in_specs = (P("ctx", "head"), P("ctx", "head"), P("ctx", "head"), P("ctx"), P("head", None))
    out_specs = P("head", "ctx")
    return jax.shard_map(body, mesh=mesh, in_specs=in_specs, out_specs=out_specs, check_vma=False)
```

```python
import functools

import jax
import jax.numpy as jnp
from jax import lax
from jax.experimental import pallas as pl
from jax.experimental.pallas import tpu as pltpu
from jax.sharding import PartitionSpec as P

SCALE = 0.08838834764831845
LOG2E = 1.4426950408889634
C = SCALE * LOG2E
NEG = -1e30
HIDE = 1e30
ROWS = 512
SPAN = 256
PARTS = 4
PART = ROWS // PARTS
OFFSETS = (4, 3, -3, 2, -2, 1, -1, 0)
f32 = jnp.float32
bf16 = jnp.bfloat16
MESH = pl.DeviceIdType.MESH


def kernel(
    q_hbm, k_hbm, v_hbm, pos_hbm, w_hbm, out_ref,
    q_ref, pos_ref, kv, posb, qT, scores, top, shift, total, acc, w_own, wT, w_oth, a_own, a_oth,
    z_out, z_in, z_out4, z_in4,
    load_sem, kv_send, kv_recv, kv_cross, pos_send, pos_recv, w_send, w_recv, w_cross,
    a_send, a_recv, z_send, z_recv,
):
    ctx = lax.axis_index("ctx")
    head = lax.axis_index("head")
    core = lax.rem(ctx, 2)
    y = lax.rem(lax.div(ctx, 2), 4)
    xh = lax.div(ctx, 8)
    z = lax.div(head, 2)
    xl = lax.rem(head, 2)
    x = xh * 2 + xl

    def device(dx, dy, dz, dcore):
        nx = lax.rem(x + dx + 4, 4)
        ny = lax.rem(y + dy + 4, 4)
        nz = lax.rem(z + dz + 8, 8)
        nc = lax.rem(core + dcore, 2)
        return {"ctx": (lax.div(nx, 2) * 4 + ny) * 2 + nc, "head": nz * 2 + lax.rem(nx, 2)}

    def first(d):
        return device(core * d, (1 - core) * d, 0, 0)

    def second(d):
        return device((1 - core) * d, core * d, 0, 0)

    other_core = device(0, 0, 0, 1)
    mate = device(1 - 2 * xl, 0, 0, 0)

    def piece_of(f, s, lane):
        own = core if lane == 0 else 1 - core
        px = lax.rem(x + own * f + (1 - own) * s, 4)
        py = lax.rem(y + (1 - own) * f + own * s, 4)
        return (lax.div(px, 2) * 4 + py) * 2 + own, lax.rem(px, 2)

    def block_of(other_hi, dy, lane):
        own = core if lane == 0 else 1 - core
        bh = 1 - xh if other_hi else xh
        return (bh * 4 + lax.rem(y + dy + 4, 4)) * 2 + own

    def remote(src, dst, send_sem, recv_sem, target):
        return pltpu.make_async_remote_copy(
            src_ref=src, dst_ref=dst, send_sem=send_sem, recv_sem=recv_sem,
            device_id=target, device_id_type=MESH,
        )

    def send(src, dst, send_sem, recv_sem, target):
        remote(src, dst, send_sem, recv_sem, target).start()

    def sent_off(src, send_sem):
        remote(src, src, send_sem, load_sem.at[0], other_core).wait_send()

    def arrived(dst, recv_sem):
        remote(dst, dst, load_sem.at[0], recv_sem, other_core).wait_recv()

    loads = []

    def load(src, dst):
        copy = pltpu.make_async_copy(src, dst, load_sem.at[len(loads)])
        copy.start()
        loads.append(copy)

    my_block = block_of(False, 0, 0)
    load(k_hbm, kv.at[my_block, xl, pl.ds(0, 64)])
    load(v_hbm, kv.at[my_block, xl, pl.ds(64, 64)])
    load(pos_hbm, pos_ref)
    load(q_hbm, q_ref)
    load(w_hbm, w_own)

    barrier = pltpu.get_barrier_semaphore()
    relations = [
        (h, dy, c) for h in range(2) for dy in range(4) for c in range(2) if (h, dy, c) != (0, 0, 0)
    ]
    friends = [device(2 * h, dy, 0, c) for h, dy, c in relations]
    friends += [device(1, 0, 0, 0), device(-1, 0, 0, 0), device(0, 0, 1, 0), device(0, 0, -1, 0)]
    for friend in friends:
        pl.semaphore_signal(barrier, inc=1, device_id=friend, device_id_type=MESH)
    for i in range(3):
        loads[i].wait()
    lane = lax.broadcasted_iota(jnp.int32, (1, 128), 1)
    posb[my_block, :, 0:128] = pos_ref[:, 0:128] - lane
    posb[my_block, :, 128:256] = pos_ref[:, SPAN : SPAN + 128] - lane
    pl.semaphore_wait(barrier, len(friends))

    passed = []

    def view_of(f, s, half):
        block, side = piece_of(f, s, 0)
        return kv.at[block, side] if half is None else kv.at[block, side, pl.ds(64 * half, 64)]

    def pass_on(f, s, target, f_there, s_there, half=None):
        view = view_of(f, s, half)
        send(view, view, kv_send.at[len(passed)],
             kv_recv.at[f_there % 4, s_there % 4, 0 if half is None else half], target)
        passed.append((f, s, half))

    def cross(f, s):
        view = view_of(f, s, None)
        send(view, view, kv_send.at[len(passed)], kv_cross.at[f, s], other_core)
        passed.append((f, s, None))

    def to_second(f):
        pass_on(f, 0, second(1), f, -1)
        pass_on(f, 0, second(-1), f, 1)

    def wait_piece(f, s):
        block, side = piece_of(f, s, 0)
        if s == 2 or (f, s) == (2, 0):
            for half in range(2):
                arrived(kv.at[block, side, pl.ds(64 * half, 64)], kv_recv.at[f, s, half])
        else:
            arrived(kv.at[block, side], kv_recv.at[f, s, 0])
        if s == 0:
            to_second(f)
        elif s == 3:
            pass_on(f, s, second(1), f, 2, half=0)
        elif s == 1:
            pass_on(f, s, second(-1), f, 2, half=1)
        cross(f, s)

    def wait_cross(f, s):
        block, side = piece_of(f, s, 1)
        arrived(kv.at[block, side], kv_cross.at[f, s])

    pass_on(0, 0, first(1), -1, 0)
    pass_on(0, 0, first(-1), 1, 0)
    pass_on(0, 0, first(2), 2, 0, half=0)
    pass_on(0, 0, first(-2), 2, 0, half=1)
    to_second(0)
    cross(0, 0)
    for i, (h, dy, c) in enumerate(relations):
        there = relations.index((h, (4 - dy) % 4, c))
        send(posb.at[my_block], posb.at[my_block], pos_send.at[i], pos_recv.at[there],
             device(2 * h, dy, 0, c))

    def weights_out(j):
        for side, d in ((0, 1), (1, -1)):
            slot = 4 * j + 2 * side + core
            offset = sum(
                (jnp.where(slot == i, o, 0) for i, o in enumerate(OFFSETS)), jnp.int32(0)
            )
            tile = lax.rem(z + offset + 8, 8) * 2 + 1 - xl
            send(wT.at[tile], w_oth.at[slot], w_send.at[j, side, 0], w_recv.at[j, side],
                 device(d, 0, 0, 0))

    def weights_in(j):
        for side in range(2):
            slot = 4 * j + 2 * side + core
            arrived(w_oth.at[slot], w_recv.at[j, side])
            send(w_oth.at[slot], w_oth.at[slot], w_send.at[j, side, 1], w_cross.at[j, side], other_core)

    def weights_crossed(j):
        for side in range(2):
            arrived(w_oth.at[4 * j + 2 * side + 1 - core], w_cross.at[j, side])

    loads[4].wait()
    for tile in range(16):
        wT[tile] = w_own[:, tile * 256 : (tile + 1) * 256].T
    loads[3].wait()
    for h in range(2):
        t = q_ref[:, h * 128 : (h + 1) * 128].T
        gap = jnp.zeros((64, ROWS), bf16)
        qT[h] = jnp.concatenate([t[:64], gap, t[64:], gap], axis=0)
    top[...] = jnp.full(top.shape, NEG, f32)
    total[...] = jnp.zeros(total.shape, f32)
    acc[...] = jnp.zeros(acc.shape, f32)

    row_pos = pos_ref[...]

    def stage_a(n, block, own):
        par = n % 2
        k = jnp.concatenate([kv[block, 0], kv[block, 1]], axis=0).T
        starts = [
            jnp.concatenate([posb[block, :, j * 128 : (j + 1) * 128]] * 4, axis=1) for j in range(2)
        ]
        seen = [start <= row_pos for start in starts]
        if own:
            inside = lax.broadcasted_iota(jnp.int32, (SPAN, ROWS), 0)
            masks = [inside + start <= row_pos for start in starts]
        for h in range(2):
            s = jnp.dot(k, qT[h], preferred_element_type=f32)
            if own:
                s = jnp.concatenate(
                    [jnp.where(masks[j], s[j * SPAN : (j + 1) * SPAN], NEG) for j in range(2)], axis=0
                )
            scores[par, h] = s
            new = top[par, h]
            for j in range(2):
                most = jnp.max(s[j * SPAN : (j + 1) * SPAN], axis=0, keepdims=True)
                new = jnp.maximum(new, jnp.where(seen[j], most, NEG))
            top[1 - par, h] = new
            for j in range(2):
                shift[par, h, j] = new * C + jnp.where(seen[j], 0.0, HIDE)

    def stage_b(n, block, fades):
        par = n % 2
        v = jnp.concatenate([kv[block, 0, 64:], kv[block, 1, 64:]], axis=0)
        for h in range(2):
            fade = fades[h]
            expo = [
                jnp.exp2(scores[par, h, j * SPAN : (j + 1) * SPAN] * C - shift[par, h, j])
                for j in range(2)
            ]
            total[h] = total[h] * fade + (
                jnp.sum(expo[0], axis=0, keepdims=True) + jnp.sum(expo[1], axis=0, keepdims=True)
            )
            weights = jnp.concatenate(expo, axis=0).astype(bf16)
            acc[h] = acc[h] * fade + jnp.dot(v, weights, preferred_element_type=f32)

    def fades_of(n):
        par = n % 2
        return [jnp.exp2((top[par, h] - top[1 - par, h]) * C) for h in range(2)]

    groups = (
        ((1, 0), (3, 0), (2, 0), (0, 1), (0, 3)),
        ((1, 1), (1, 3)),
        ((3, 1), (3, 3)),
        ((2, 1), (2, 3)),
        ((0, 2),),
        ((1, 2),),
        ((3, 2),),
        ((2, 2),),
    )
    orders = ((0, 1, 3, 2, 4, 5, 7, 6), (0, 4, 1, 3, 5, 7, 2, 6))

    def nth_block(n, which):
        number = core if which == 0 else 1 - core
        code = jnp.int32(0)
        for i in range(1, 8):
            code = code + jnp.where(n == i, orders[0][i] + number * (orders[1][i] - orders[0][i]), 0)
        bh = lax.rem(xh + lax.div(code, 4), 2)
        return (bh * 4 + lax.rem(y + lax.rem(code, 4), 4)) * 2 + number

    def own_group(g):
        for f, s in groups[g]:
            wait_piece(f, s)
        if g == 3:
            weights_out(0)

    def cross_group(g):
        for f, s in (((0, 0),) if g == 0 else ()) + groups[g]:
            wait_cross(f, s)

    def a_beside_b(n, block, before):
        fades = fades_of(n - 1)
        stage_a(n, block, False)
        stage_b(n - 1, before, fades)

    own_group(0)
    stage_a(0, my_block, True)
    for i, (h, dy, c) in enumerate(relations):
        block = (lax.rem(xh + h, 2) * 4 + lax.rem(y + dy, 4)) * 2 + lax.rem(core + c, 2)
        arrived(posb.at[block], pos_recv.at[i])

    def two_blocks(j, carry):
        for g in range(7):
            @pl.when(j == g)
            def comm(g=g):
                own_group(g + 1)
                cross_group(g)
        a_beside_b(1, nth_block(j, 1), nth_block(j, 0))
        a_beside_b(2, nth_block(j + 1, 0), nth_block(j, 1))
        return carry

    lax.fori_loop(0, 7, two_blocks, 0)
    cross_group(7)
    a_beside_b(1, nth_block(7, 1), nth_block(7, 0))
    stage_b(1, nth_block(7, 1), fades_of(1))

    for t in range(PARTS):
        cols = slice(t * PART, (t + 1) * PART)
        for h in range(2):
            scale = 1.0 / total[h, :, cols]
            a_own[t, h * 128 : (h + 1) * 128, :] = (acc[h, :, cols] * scale).astype(bf16)
        send(a_own.at[t], a_oth.at[t], a_send.at[t], a_recv.at[t], mate)

    weights_in(0)
    weights_crossed(0)

    def project(offset, t):
        tile = lax.rem(z + offset + 8, 8) * 2 + xl
        return jnp.dot(wT[tile], a_own[t], preferred_element_type=f32) + jnp.dot(
            w_oth[OFFSETS.index(offset)], a_oth[t], preferred_element_type=f32
        )

    def up_and_down():
        return ((0, 1), (1, -1))

    def farthest(t, carry):
        arrived(a_oth.at[t], a_recv.at[t])
        part = project(4, t)
        for d, sign in up_and_down():
            z_out4[d, t] = part[d * 128 : (d + 1) * 128].astype(bf16)
            send(z_out4.at[d, t], z_in4.at[d, t], z_send.at[d, 3, t], z_recv.at[d, 3, t],
                 device(0, 0, sign, 0))
        return carry

    def third(t, carry):
        for d, sign in up_and_down():
            part = project(sign * 3, t)
            arrived(z_in4.at[d, t], z_recv.at[d, 3, t])
            more = part[d * 128 : (d + 1) * 128] + z_in4[d, t].astype(f32)
            rest = part[(1 - d) * 128 : (2 - d) * 128]
            z_out[d, 2, t, d * 128 : (d + 1) * 128, :] = more.astype(bf16)
            z_out[d, 2, t, (1 - d) * 128 : (2 - d) * 128, :] = rest.astype(bf16)
            send(z_out.at[d, 2, t], z_in.at[d, 2, t], z_send.at[d, 2, t], z_recv.at[d, 2, t],
                 device(0, 0, sign, 0))
        return carry

    def nearer(k, t, carry):
        for d, sign in up_and_down():
            part = project(sign * k, t)
            arrived(z_in.at[d, k, t], z_recv.at[d, k, t])
            z_out[d, k - 1, t] = (part + z_in[d, k, t].astype(f32)).astype(bf16)
            send(z_out.at[d, k - 1, t], z_in.at[d, k - 1, t], z_send.at[d, k - 1, t],
                 z_recv.at[d, k - 1, t], device(0, 0, sign, 0))
        return carry

    lax.fori_loop(0, PARTS, farthest, 0)
    weights_out(1)
    lax.fori_loop(0, PARTS, third, 0)
    weights_in(1)
    weights_crossed(1)
    lax.fori_loop(0, PARTS, functools.partial(nearer, 2), 0)
    lax.fori_loop(0, PARTS, functools.partial(nearer, 1), 0)
    for t in range(PARTS):
        part = project(0, t)
        for d in range(2):
            arrived(z_in.at[d, 0, t], z_recv.at[d, 0, t])
        out_ref[:, t * PART : (t + 1) * PART] = (
            part + (z_in[0, 0, t].astype(f32) + z_in[1, 0, t].astype(f32))
        ).astype(bf16)

    for i, (f, s, half) in enumerate(passed):
        sent_off(view_of(f, s, half), kv_send.at[i])
    for i in range(len(relations)):
        sent_off(posb.at[my_block], pos_send.at[i])
    for j in range(2):
        for side in range(2):
            for leg in range(2):
                sent_off(wT.at[0], w_send.at[j, side, leg])
    for t in range(PARTS):
        sent_off(a_own.at[t], a_send.at[t])
        for d in range(2):
            sent_off(z_out4.at[d, t], z_send.at[d, 3, t])
            for k in range(3):
                sent_off(z_out.at[d, k, t], z_send.at[d, k, t])


def body(queries, keys, values, positions, out_weight):
    hbm = pl.BlockSpec(memory_space=pltpu.HBM)
    dma = pltpu.SemaphoreType.DMA
    return pl.pallas_call(
        kernel,
        out_shape=jax.ShapeDtypeStruct((256, ROWS), bf16),
        in_specs=[hbm] * 5,
        out_specs=pl.BlockSpec(memory_space=pltpu.VMEM),
        scratch_shapes=[
            pltpu.VMEM((ROWS, 256), bf16),
            pltpu.VMEM((1, ROWS), jnp.int32),
            pltpu.VMEM((16, 2, 128, ROWS), bf16),
            pltpu.VMEM((16, 1, 256), jnp.int32),
            pltpu.VMEM((2, 256, ROWS), bf16),
            pltpu.VMEM((2, 2, ROWS, ROWS), f32),
            pltpu.VMEM((2, 2, 1, ROWS), f32),
            pltpu.VMEM((2, 2, 2, 1, ROWS), f32),
            pltpu.VMEM((2, 1, ROWS), f32),
            pltpu.VMEM((2, 128, ROWS), f32),
            pltpu.VMEM((256, 4096), bf16),
            pltpu.VMEM((16, 256, 256), bf16),
            pltpu.VMEM((8, 256, 256), bf16),
            pltpu.VMEM((PARTS, 256, PART), bf16),
            pltpu.VMEM((PARTS, 256, PART), bf16),
            pltpu.VMEM((2, 3, PARTS, 256, PART), bf16),
            pltpu.VMEM((2, 3, PARTS, 256, PART), bf16),
            pltpu.VMEM((2, PARTS, 128, PART), bf16),
            pltpu.VMEM((2, PARTS, 128, PART), bf16),
            dma((5,)),
            dma((36,)),
            dma((4, 4, 2)),
            dma((4, 4)),
            dma((15,)),
            dma((15,)),
            dma((2, 2, 2)),
            dma((2, 2)),
            dma((2, 2)),
            dma((PARTS,)),
            dma((PARTS,)),
            dma((2, 4, PARTS)),
            dma((2, 4, PARTS)),
        ],
        compiler_params=pltpu.CompilerParams(
            collective_id=0, has_side_effects=True, vmem_limit_bytes=56 << 20
        ),
        cost_estimate=pl.CostEstimate(flops=6_000_000_000, bytes_accessed=4_000_000, transcendentals=8_400_000),
    )(queries, keys.T, values.T, positions.reshape(1, ROWS), out_weight)


def solution(mesh):
    in_specs = (P("ctx", "head"), P("ctx", "head"), P("ctx", "head"), P("ctx"), P("head", None))
    out_specs = P("head", "ctx")
    return jax.shard_map(body, mesh=mesh, in_specs=in_specs, out_specs=out_specs, check_vma=False)
```

```python
import functools

import jax
import jax.numpy as jnp
from jax import lax
from jax.experimental import pallas as pl
from jax.experimental.pallas import tpu as pltpu
from jax.sharding import PartitionSpec as P

SCALE = 0.08838834764831845
LOG2E = 1.4426950408889634
C = SCALE * LOG2E
NEG = -1e30
HIDE = 1e30
ROWS = 512
SPAN = 256
PARTS = 4
PART = ROWS // PARTS
TILE = 256
OFFSETS = (4, 3, -3, 2, -2, 1, -1, 0)
f32 = jnp.float32
bf16 = jnp.bfloat16
MESH = pl.DeviceIdType.MESH


def kernel(
    q_hbm, k_hbm, v_hbm, pos_hbm, w_hbm, out_ref,
    q_ref, pos_ref, kv, posb, qT, scores, top, shift, total, acc, w_own, wT, w_oth, a_own, a_oth,
    z_out, z_in, z_out4, z_in4,
    load_sem, kv_send, kv_recv, kv_cross, pos_send, pos_recv, w_send, w_recv, w_cross,
    a_send, a_recv, z_send, z_recv,
):
    ctx = lax.axis_index("ctx")
    head = lax.axis_index("head")
    core = ctx & 1
    y = (ctx >> 1) & 3
    xh = ctx >> 3
    z = head >> 1
    xl = head & 1
    x = xh * 2 + xl

    def device(dx, dy, dz, dcore):
        nx = (x + dx) & 3
        ny = (y + dy) & 3
        nz = (z + dz) & 7
        nc = (core + dcore) & 1
        return {"ctx": ((nx >> 1) * 4 + ny) * 2 + nc, "head": nz * 2 + (nx & 1)}

    firsts = {d: device(core * d, (1 - core) * d, 0, 0) for d in (-2, -1, 1, 2)}
    seconds = {d: device((1 - core) * d, core * d, 0, 0) for d in (-1, 1)}
    first = firsts.get
    second = seconds.get

    other_core = device(0, 0, 0, 1)
    mate = device(1 - 2 * xl, 0, 0, 0)
    along = (device(0, 0, 1, 0), device(0, 0, -1, 0))

    def piece_of(f, s, lane):
        own = core if lane == 0 else 1 - core
        px = (x + s + own * (f - s)) & 3
        py = (y + f + own * (s - f)) & 3
        return ((px >> 1) * 4 + py) * 2 + own, px & 1

    def remote(src, dst, send_sem, recv_sem, target):
        return pltpu.make_async_remote_copy(
            src_ref=src, dst_ref=dst, send_sem=send_sem, recv_sem=recv_sem,
            device_id=target, device_id_type=MESH,
        )

    def send(src, dst, send_sem, recv_sem, target):
        remote(src, dst, send_sem, recv_sem, target).start()

    def sent_off(src, send_sem):
        remote(src, src, send_sem, load_sem.at[0], other_core).wait_send()

    def arrived(dst, recv_sem):
        remote(dst, dst, load_sem.at[0], recv_sem, other_core).wait_recv()

    loads = []

    def load(src, dst):
        copy = pltpu.make_async_copy(src, dst, load_sem.at[len(loads)])
        copy.start()
        loads.append(copy)

    my_block = ctx
    load(k_hbm, kv.at[my_block, xl, pl.ds(0, 64)])
    load(v_hbm, kv.at[my_block, xl, pl.ds(64, 64)])
    load(pos_hbm, pos_ref)
    load(q_hbm, q_ref)
    load(w_hbm, w_own)

    barrier = pltpu.get_barrier_semaphore()
    relations = [
        (h, dy, c) for h in range(2) for dy in range(4) for c in range(2) if (h, dy, c) != (0, 0, 0)
    ]
    friends = [device(2 * h, dy, 0, c) for h, dy, c in relations]
    friends += [device(1, 0, 0, 0), device(-1, 0, 0, 0), device(0, 0, 1, 0), device(0, 0, -1, 0)]
    for friend in friends:
        pl.semaphore_signal(barrier, inc=1, device_id=friend, device_id_type=MESH)
    for i in range(3):
        loads[i].wait()
    lane = lax.broadcasted_iota(jnp.int32, (1, 128), 1)
    posb[my_block, :, 0:128] = pos_ref[:, 0:128] - lane
    posb[my_block, :, 128:256] = pos_ref[:, SPAN : SPAN + 128] - lane
    pl.semaphore_wait(barrier, len(friends))

    passed = []

    def view_of(f, s, half):
        block, side = piece_of(f, s, 0)
        return kv.at[block, side] if half is None else kv.at[block, side, pl.ds(64 * half, 64)]

    def pass_on(f, s, target, f_there, s_there, half=None):
        view = view_of(f, s, half)
        send(view, view, kv_send.at[len(passed)],
             kv_recv.at[f_there % 4, s_there % 4, 0 if half is None else half], target)
        passed.append((f, s, half))

    def cross(f, s):
        view = view_of(f, s, None)
        send(view, view, kv_send.at[len(passed)], kv_cross.at[f, s], other_core)
        passed.append((f, s, None))

    def to_second(f):
        pass_on(f, 0, second(1), f, -1)
        pass_on(f, 0, second(-1), f, 1)

    def wait_piece(f, s):
        block, side = piece_of(f, s, 0)
        if s == 2 or (f, s) == (2, 0):
            for half in range(2):
                arrived(kv.at[block, side, pl.ds(64 * half, 64)], kv_recv.at[f, s, half])
        else:
            arrived(kv.at[block, side], kv_recv.at[f, s, 0])
        if s == 0:
            to_second(f)
        elif s == 3:
            pass_on(f, s, second(1), f, 2, half=0)
        elif s == 1:
            pass_on(f, s, second(-1), f, 2, half=1)
        cross(f, s)

    def wait_cross(f, s):
        block, side = piece_of(f, s, 1)
        arrived(kv.at[block, side], kv_cross.at[f, s])

    pass_on(0, 0, first(1), -1, 0)
    pass_on(0, 0, first(-1), 1, 0)
    pass_on(0, 0, first(2), 2, 0, half=0)
    pass_on(0, 0, first(-2), 2, 0, half=1)
    to_second(0)
    cross(0, 0)
    for i, (h, dy, c) in enumerate(relations):
        there = relations.index((h, (4 - dy) % 4, c))
        send(posb.at[my_block], posb.at[my_block], pos_send.at[i], pos_recv.at[there],
             device(2 * h, dy, 0, c))

    def weights_out(j):
        for side, d in ((0, 1), (1, -1)):
            slot = 4 * j + 2 * side + core
            offset = sum(
                (jnp.where(slot == i, o, 0) for i, o in enumerate(OFFSETS)), jnp.int32(0)
            )
            tile = ((z + offset) & 7) * 2 + 1 - xl
            send(wT.at[tile], w_oth.at[slot], w_send.at[j, side, 0], w_recv.at[j, side],
                 device(d, 0, 0, 0))

    def weights_in(j):
        for side in range(2):
            slot = 4 * j + 2 * side + core
            arrived(w_oth.at[slot], w_recv.at[j, side])
            send(w_oth.at[slot], w_oth.at[slot], w_send.at[j, side, 1], w_cross.at[j, side], other_core)

    def weights_crossed(j):
        for side in range(2):
            arrived(w_oth.at[4 * j + 2 * side + 1 - core], w_cross.at[j, side])

    loads[4].wait()
    for tile in range(16):
        wT[tile] = w_own[:, tile * 256 : (tile + 1) * 256].T
    loads[3].wait()
    for h in range(2):
        t = q_ref[:, h * 128 : (h + 1) * 128].T
        gap = jnp.zeros((64, ROWS), bf16)
        qT[h] = jnp.concatenate([t[:64], gap, t[64:], gap], axis=0)
    top[...] = jnp.full(top.shape, NEG, f32)
    total[...] = jnp.zeros(total.shape, f32)
    acc[...] = jnp.zeros(acc.shape, f32)

    row_pos = pos_ref[...]

    def starts_of(block):
        return [
            jnp.concatenate([posb[block, :, j * 128 : (j + 1) * 128]] * 4, axis=1) for j in range(2)
        ]

    def part_a(par, h, cols, k, seen, masks):
        s = jnp.dot(k, qT[h, :, cols], preferred_element_type=f32)
        if masks is not None:
            s = jnp.concatenate(
                [jnp.where(masks[j][:, cols], s[j * SPAN : (j + 1) * SPAN], NEG) for j in range(2)], axis=0
            )
        scores[par, h, :, cols] = s
        new = top[par, h, :, cols]
        for j in range(2):
            most = jnp.max(s[j * SPAN : (j + 1) * SPAN], axis=0, keepdims=True)
            new = jnp.maximum(new, jnp.where(seen[j][:, cols], most, NEG))
        top[1 - par, h, :, cols] = new
        for j in range(2):
            shift[par, h, j, :, cols] = new * C + jnp.where(seen[j][:, cols], 0.0, HIDE)

    def part_b(par, h, cols, v, fade):
        expo = [
            jnp.exp2(scores[par, h, j * SPAN : (j + 1) * SPAN, cols] * C - shift[par, h, j, :, cols])
            for j in range(2)
        ]
        total[h, :, cols] = total[h, :, cols] * fade + (
            jnp.sum(expo[0], axis=0, keepdims=True) + jnp.sum(expo[1], axis=0, keepdims=True)
        )
        more = jnp.dot(v, jnp.concatenate(expo, axis=0).astype(bf16), preferred_element_type=f32)
        acc[h, :, cols] = acc[h, :, cols] * fade + more

    tiles = [(h, slice(r * TILE, (r + 1) * TILE)) for r in range(ROWS // TILE) for h in range(2)]

    def keys_of(block):
        return jnp.concatenate([kv[block, 0], kv[block, 1]], axis=0).T

    def values_of(block):
        return jnp.concatenate([kv[block, 0, 64:], kv[block, 1, 64:]], axis=0)

    def fade_of(n, h, cols):
        par = n % 2
        return jnp.exp2((top[par, h, :, cols] - top[1 - par, h, :, cols]) * C)

    groups = (
        ((1, 0), (3, 0), (2, 0), (0, 1), (0, 3)),
        ((1, 1), (1, 3)),
        ((3, 1), (3, 3)),
        ((2, 1), (2, 3)),
        ((0, 2),),
        ((1, 2),),
        ((3, 2),),
        ((2, 2),),
    )
    orders = ((0, 1, 3, 2, 4, 5, 7, 6), (0, 4, 1, 3, 5, 7, 2, 6))

    coded = [sum(code << (3 * i) for i, code in enumerate(order)) for order in orders]

    def nth_block(n, which):
        number = core if which == 0 else 1 - core
        code = ((coded[0] + number * (coded[1] - coded[0])) >> (3 * n)) & 7
        return ((((xh + (code >> 2)) & 1) * 4) + ((y + code) & 3)) * 2 + number

    def own_group(g):
        for f, s in groups[g]:
            wait_piece(f, s)
        if g == 3:
            weights_out(0)

    def cross_group(g):
        for f, s in (((0, 0),) if g == 0 else ()) + groups[g]:
            wait_cross(f, s)

    def a_beside_b(n, block, before, then=None):
        seen = [start <= row_pos for start in starts_of(block)]
        k, v = keys_of(block), values_of(before)
        for h, cols in tiles:
            fade = fade_of(n - 1, h, cols)
            part_a(n % 2, h, cols, k, seen, None)
            part_b((n - 1) % 2, h, cols, v, fade)
            if then is not None:
                then(h, cols)

    own_group(0)
    starts = starts_of(my_block)
    inside = lax.broadcasted_iota(jnp.int32, (SPAN, ROWS), 0)
    masks = [inside + start <= row_pos for start in starts]
    own_keys = keys_of(my_block)
    for h, cols in tiles:
        part_a(0, h, cols, own_keys, [start <= row_pos for start in starts], masks)
    for i, (h, dy, c) in enumerate(relations):
        block = (((xh + h) & 1) * 4 + ((y + dy) & 3)) * 2 + ((core + c) & 1)
        arrived(posb.at[block], pos_recv.at[i])

    def two_blocks(j, carry):
        for g in range(7):
            @pl.when(j == g)
            def comm(g=g):
                own_group(g + 1)
                cross_group(g)
        a_beside_b(1, nth_block(j, 1), nth_block(j, 0))
        a_beside_b(2, nth_block(j + 1, 0), nth_block(j, 1))
        return carry

    lax.fori_loop(0, 7, two_blocks, 0)
    cross_group(7)
    last_values = values_of(nth_block(7, 1))

    def finish(h, cols):
        part_b(1, h, cols, last_values, fade_of(1, h, cols))
        scale = 1.0 / total[h, :, cols]
        done = (acc[h, :, cols] * scale).astype(bf16)
        for i in range(TILE // PART):
            t = cols.start // PART + i
            a_own[t, h * 128 : (h + 1) * 128, :] = done[:, i * PART : (i + 1) * PART]
            if h == 1:
                send(a_own.at[t], a_oth.at[t], a_send.at[t], a_recv.at[t], mate)

    a_beside_b(1, nth_block(7, 1), nth_block(7, 0), finish)

    weights_in(0)
    weights_crossed(0)

    def project(offset, t):
        tile = ((z + offset) & 7) * 2 + xl
        return jnp.dot(wT[tile], a_own[t], preferred_element_type=f32) + jnp.dot(
            w_oth[OFFSETS.index(offset)], a_oth[t], preferred_element_type=f32
        )

    def up_and_down():
        return ((0, 1), (1, -1))

    def farthest(t, carry):
        arrived(a_oth.at[t], a_recv.at[t])
        part = project(4, t)
        for d, sign in up_and_down():
            z_out4[d, t] = part[d * 128 : (d + 1) * 128].astype(bf16)
            send(z_out4.at[d, t], z_in4.at[d, t], z_send.at[d, 3, t], z_recv.at[d, 3, t], along[d])
        return carry

    def third(t, carry):
        for d, sign in up_and_down():
            part = project(sign * 3, t)
            arrived(z_in4.at[d, t], z_recv.at[d, 3, t])
            more = part[d * 128 : (d + 1) * 128] + z_in4[d, t].astype(f32)
            rest = part[(1 - d) * 128 : (2 - d) * 128]
            z_out[d, 2, t, d * 128 : (d + 1) * 128, :] = more.astype(bf16)
            z_out[d, 2, t, (1 - d) * 128 : (2 - d) * 128, :] = rest.astype(bf16)
            send(z_out.at[d, 2, t], z_in.at[d, 2, t], z_send.at[d, 2, t], z_recv.at[d, 2, t], along[d])
        return carry

    def nearer(k, t, carry):
        for d, sign in up_and_down():
            part = project(sign * k, t)
            arrived(z_in.at[d, k, t], z_recv.at[d, k, t])
            z_out[d, k - 1, t] = (part + z_in[d, k, t].astype(f32)).astype(bf16)
            send(z_out.at[d, k - 1, t], z_in.at[d, k - 1, t], z_send.at[d, k - 1, t],
                 z_recv.at[d, k - 1, t], along[d])
        return carry

    lax.fori_loop(0, PARTS, farthest, 0)
    weights_out(1)
    lax.fori_loop(0, PARTS, third, 0)
    weights_in(1)
    weights_crossed(1)
    lax.fori_loop(0, PARTS, functools.partial(nearer, 2), 0)
    lax.fori_loop(0, PARTS, functools.partial(nearer, 1), 0)
    for t in range(PARTS):
        part = project(0, t)
        for d in range(2):
            arrived(z_in.at[d, 0, t], z_recv.at[d, 0, t])
        out_ref[:, t * PART : (t + 1) * PART] = (
            part + (z_in[0, 0, t].astype(f32) + z_in[1, 0, t].astype(f32))
        ).astype(bf16)

    for i, (f, s, half) in enumerate(passed):
        sent_off(view_of(f, s, half), kv_send.at[i])
    for i in range(len(relations)):
        sent_off(posb.at[my_block], pos_send.at[i])
    for j in range(2):
        for side in range(2):
            for leg in range(2):
                sent_off(wT.at[0], w_send.at[j, side, leg])
    for t in range(PARTS):
        sent_off(a_own.at[t], a_send.at[t])
        for d in range(2):
            sent_off(z_out4.at[d, t], z_send.at[d, 3, t])
            for k in range(3):
                sent_off(z_out.at[d, k, t], z_send.at[d, k, t])


def body(queries, keys, values, positions, out_weight):
    hbm = pl.BlockSpec(memory_space=pltpu.HBM)
    dma = pltpu.SemaphoreType.DMA
    return pl.pallas_call(
        kernel,
        out_shape=jax.ShapeDtypeStruct((256, ROWS), bf16),
        in_specs=[hbm] * 5,
        out_specs=pl.BlockSpec(memory_space=pltpu.VMEM),
        scratch_shapes=[
            pltpu.VMEM((ROWS, 256), bf16),
            pltpu.VMEM((1, ROWS), jnp.int32),
            pltpu.VMEM((16, 2, 128, ROWS), bf16),
            pltpu.VMEM((16, 1, 256), jnp.int32),
            pltpu.VMEM((2, 256, ROWS), bf16),
            pltpu.VMEM((2, 2, ROWS, ROWS), f32),
            pltpu.VMEM((2, 2, 1, ROWS), f32),
            pltpu.VMEM((2, 2, 2, 1, ROWS), f32),
            pltpu.VMEM((2, 1, ROWS), f32),
            pltpu.VMEM((2, 128, ROWS), f32),
            pltpu.VMEM((256, 4096), bf16),
            pltpu.VMEM((16, 256, 256), bf16),
            pltpu.VMEM((8, 256, 256), bf16),
            pltpu.VMEM((PARTS, 256, PART), bf16),
            pltpu.VMEM((PARTS, 256, PART), bf16),
            pltpu.VMEM((2, 3, PARTS, 256, PART), bf16),
            pltpu.VMEM((2, 3, PARTS, 256, PART), bf16),
            pltpu.VMEM((2, PARTS, 128, PART), bf16),
            pltpu.VMEM((2, PARTS, 128, PART), bf16),
            dma((5,)),
            dma((36,)),
            dma((4, 4, 2)),
            dma((4, 4)),
            dma((15,)),
            dma((15,)),
            dma((2, 2, 2)),
            dma((2, 2)),
            dma((2, 2)),
            dma((PARTS,)),
            dma((PARTS,)),
            dma((2, 4, PARTS)),
            dma((2, 4, PARTS)),
        ],
        compiler_params=pltpu.CompilerParams(
            collective_id=0, has_side_effects=True, vmem_limit_bytes=56 << 20
        ),
        cost_estimate=pl.CostEstimate(flops=6_000_000_000, bytes_accessed=4_000_000, transcendentals=8_400_000),
    )(queries, keys.T, values.T, positions.reshape(1, ROWS), out_weight)


def solution(mesh):
    in_specs = (P("ctx", "head"), P("ctx", "head"), P("ctx", "head"), P("ctx"), P("head", None))
    out_specs = P("head", "ctx")
    return jax.shard_map(body, mesh=mesh, in_specs=in_specs, out_specs=out_specs, check_vma=False)
```

```python
import functools

import jax
import jax.numpy as jnp
from jax import lax
from jax.experimental import pallas as pl
from jax.experimental.pallas import tpu as pltpu
from jax.sharding import PartitionSpec as P

SCALE = 0.08838834764831845
LOG2E = 1.4426950408889634
C = SCALE * LOG2E
NEG = -1e30
HIDE = 1e30
ROWS = 512
SPAN = 256
PARTS = 4
PART = ROWS // PARTS
TILE = 256
OFFSETS = (4, 3, -3, 2, -2, 1, -1, 0)
f32 = jnp.float32
bf16 = jnp.bfloat16
MESH = pl.DeviceIdType.MESH


def kernel(
    q_hbm, k_hbm, v_hbm, pos_hbm, w_hbm, out_ref,
    q_ref, pos_ref, kv, posb, qT, scores, top, shift, total, acc, w_own, wT, w_oth, a_own, a_oth,
    z_out, z_in, z_out4, z_in4,
    load_sem, kv_send, kv_recv, kv_cross, pos_send, pos_recv, w_send, w_recv, w_cross,
    a_send, a_recv, z_send, z_recv,
):
    ctx = lax.axis_index("ctx")
    head = lax.axis_index("head")
    core = ctx & 1
    y = (ctx >> 1) & 3
    xh = ctx >> 3
    z = head >> 1
    xl = head & 1
    x = xh * 2 + xl

    def device(dx, dy, dz, dcore):
        nx = (x + dx) & 3
        ny = (y + dy) & 3
        nz = (z + dz) & 7
        nc = (core + dcore) & 1
        return {"ctx": ((nx >> 1) * 4 + ny) * 2 + nc, "head": nz * 2 + (nx & 1)}

    firsts = {d: device(core * d, (1 - core) * d, 0, 0) for d in (-2, -1, 1, 2)}
    seconds = {d: device((1 - core) * d, core * d, 0, 0) for d in (-1, 1)}
    first = firsts.get
    second = seconds.get

    other_core = device(0, 0, 0, 1)
    mate = device(1 - 2 * xl, 0, 0, 0)
    along = (device(0, 0, 1, 0), device(0, 0, -1, 0))

    def piece_of(f, s, lane):
        own = core if lane == 0 else 1 - core
        px = (x + s + own * (f - s)) & 3
        py = (y + f + own * (s - f)) & 3
        return ((px >> 1) * 4 + py) * 2 + own, px & 1

    def remote(src, dst, send_sem, recv_sem, target):
        return pltpu.make_async_remote_copy(
            src_ref=src, dst_ref=dst, send_sem=send_sem, recv_sem=recv_sem,
            device_id=target, device_id_type=MESH,
        )

    def send(src, dst, send_sem, recv_sem, target):
        remote(src, dst, send_sem, recv_sem, target).start()

    def sent_off(src, send_sem):
        remote(src, src, send_sem, load_sem.at[0], other_core).wait_send()

    def arrived(dst, recv_sem):
        remote(dst, dst, load_sem.at[0], recv_sem, other_core).wait_recv()

    loads = []

    def load(src, dst):
        copy = pltpu.make_async_copy(src, dst, load_sem.at[len(loads)])
        copy.start()
        loads.append(copy)

    my_block = ctx
    load(k_hbm, kv.at[my_block, xl, pl.ds(0, 64)])
    load(v_hbm, kv.at[my_block, xl, pl.ds(64, 64)])
    load(pos_hbm, pos_ref)
    load(q_hbm, q_ref)
    load(w_hbm, w_own)

    barrier = pltpu.get_barrier_semaphore()
    relations = [
        (h, dy, c) for h in range(2) for dy in range(4) for c in range(2) if (h, dy, c) != (0, 0, 0)
    ]
    friends = [device(2 * h, dy, 0, c) for h, dy, c in relations]
    friends += [device(1, 0, 0, 0), device(-1, 0, 0, 0), device(0, 0, 1, 0), device(0, 0, -1, 0)]
    for friend in friends:
        pl.semaphore_signal(barrier, inc=1, device_id=friend, device_id_type=MESH)
    for i in range(3):
        loads[i].wait()
    lane = lax.broadcasted_iota(jnp.int32, (1, 128), 1)
    posb[my_block, :, 0:128] = pos_ref[:, 0:128] - lane
    posb[my_block, :, 128:256] = pos_ref[:, SPAN : SPAN + 128] - lane
    pl.semaphore_wait(barrier, len(friends))

    passed = []

    def view_of(f, s, half):
        block, side = piece_of(f, s, 0)
        return kv.at[block, side] if half is None else kv.at[block, side, pl.ds(64 * half, 64)]

    def pass_on(f, s, target, f_there, s_there, half=None):
        view = view_of(f, s, half)
        send(view, view, kv_send.at[len(passed)],
             kv_recv.at[f_there % 4, s_there % 4, 0 if half is None else half], target)
        passed.append((f, s, half))

    def cross(f, s):
        view = view_of(f, s, None)
        send(view, view, kv_send.at[len(passed)], kv_cross.at[f, s], other_core)
        passed.append((f, s, None))

    def to_second(f):
        pass_on(f, 0, second(1), f, -1)
        pass_on(f, 0, second(-1), f, 1)

    def wait_piece(f, s):
        block, side = piece_of(f, s, 0)
        if s == 2 or (f, s) == (2, 0):
            for half in range(2):
                arrived(kv.at[block, side, pl.ds(64 * half, 64)], kv_recv.at[f, s, half])
        else:
            arrived(kv.at[block, side], kv_recv.at[f, s, 0])
        if s == 0:
            to_second(f)
        elif s == 3:
            pass_on(f, s, second(1), f, 2, half=0)
        elif s == 1:
            pass_on(f, s, second(-1), f, 2, half=1)
        cross(f, s)

    def wait_cross(f, s):
        block, side = piece_of(f, s, 1)
        arrived(kv.at[block, side], kv_cross.at[f, s])

    pass_on(0, 0, first(1), -1, 0)
    pass_on(0, 0, first(-1), 1, 0)
    pass_on(0, 0, first(2), 2, 0, half=0)
    pass_on(0, 0, first(-2), 2, 0, half=1)
    to_second(0)
    cross(0, 0)
    for i, (h, dy, c) in enumerate(relations):
        there = relations.index((h, (4 - dy) % 4, c))
        send(posb.at[my_block], posb.at[my_block], pos_send.at[i], pos_recv.at[there],
             device(2 * h, dy, 0, c))

    def weights_out(j):
        for side, d in ((0, 1), (1, -1)):
            slot = 4 * j + 2 * side + core
            offset = sum(
                (jnp.where(slot == i, o, 0) for i, o in enumerate(OFFSETS)), jnp.int32(0)
            )
            tile = ((z + offset) & 7) * 2 + 1 - xl
            send(wT.at[tile], w_oth.at[slot], w_send.at[j, side, 0], w_recv.at[j, side],
                 device(d, 0, 0, 0))

    def weights_in(j):
        for side in range(2):
            slot = 4 * j + 2 * side + core
            arrived(w_oth.at[slot], w_recv.at[j, side])
            send(w_oth.at[slot], w_oth.at[slot], w_send.at[j, side, 1], w_cross.at[j, side], other_core)

    def weights_crossed(j):
        for side in range(2):
            arrived(w_oth.at[4 * j + 2 * side + 1 - core], w_cross.at[j, side])

    loads[4].wait()
    for tile in range(16):
        wT[tile] = w_own[:, tile * 256 : (tile + 1) * 256].T
    loads[3].wait()
    for h in range(2):
        t = q_ref[:, h * 128 : (h + 1) * 128].T
        gap = jnp.zeros((64, ROWS), bf16)
        qT[h] = jnp.concatenate([t[:64], gap, t[64:], gap], axis=0)
    top[...] = jnp.full(top.shape, NEG, f32)
    total[...] = jnp.zeros(total.shape, f32)
    acc[...] = jnp.zeros(acc.shape, f32)

    row_pos = pos_ref[...]

    def starts_of(block):
        return [
            jnp.concatenate([posb[block, :, j * 128 : (j + 1) * 128]] * 4, axis=1) for j in range(2)
        ]

    def part_a(par, h, cols, k, seen, masks):
        s = jnp.dot(k, qT[h, :, cols], preferred_element_type=f32)
        if masks is not None:
            s = jnp.concatenate(
                [jnp.where(masks[j][:, cols], s[j * SPAN : (j + 1) * SPAN], NEG) for j in range(2)], axis=0
            )
        scores[par, h, :, cols] = s
        new = top[par, h, :, cols]
        for j in range(2):
            most = jnp.max(s[j * SPAN : (j + 1) * SPAN], axis=0, keepdims=True)
            new = jnp.maximum(new, jnp.where(seen[j][:, cols], most, NEG))
        top[1 - par, h, :, cols] = new
        for j in range(2):
            shift[par, h, j, :, cols] = new * C + jnp.where(seen[j][:, cols], 0.0, HIDE)

    def part_b(par, h, cols, v, fade):
        expo = [
            jnp.exp2(scores[par, h, j * SPAN : (j + 1) * SPAN, cols] * C - shift[par, h, j, :, cols])
            for j in range(2)
        ]
        total[h, :, cols] = total[h, :, cols] * fade + (
            jnp.sum(expo[0], axis=0, keepdims=True) + jnp.sum(expo[1], axis=0, keepdims=True)
        )
        more = jnp.dot(v, jnp.concatenate(expo, axis=0).astype(bf16), preferred_element_type=f32)
        acc[h, :, cols] = acc[h, :, cols] * fade + more

    tiles = [(h, slice(r * TILE, (r + 1) * TILE)) for r in range(ROWS // TILE) for h in range(2)]

    def keys_of(block):
        return jnp.concatenate([kv[block, 0], kv[block, 1]], axis=0).T

    def values_of(block):
        return jnp.concatenate([kv[block, 0, 64:], kv[block, 1, 64:]], axis=0)

    def fade_of(n, h, cols):
        par = n % 2
        return jnp.exp2((top[par, h, :, cols] - top[1 - par, h, :, cols]) * C)

    groups = (
        ((1, 0), (3, 0), (2, 0), (0, 1), (0, 3)),
        ((1, 1), (1, 3)),
        ((3, 1), (3, 3)),
        ((2, 1), (2, 3)),
        ((0, 2),),
        ((1, 2),),
        ((3, 2),),
        ((2, 2),),
    )
    orders = ((0, 1, 3, 2, 4, 5, 7, 6), (0, 4, 1, 3, 5, 7, 2, 6))

    coded = [sum(code << (3 * i) for i, code in enumerate(order)) for order in orders]

    def nth_block(n, which):
        number = core if which == 0 else 1 - core
        code = ((coded[0] + number * (coded[1] - coded[0])) >> (3 * n)) & 7
        return ((((xh + (code >> 2)) & 1) * 4) + ((y + code) & 3)) * 2 + number

    def own_group(g):
        for f, s in groups[g]:
            wait_piece(f, s)
        if g == 3:
            weights_out(0)

    def cross_group(g):
        for f, s in (((0, 0),) if g == 0 else ()) + groups[g]:
            wait_cross(f, s)

    def a_beside_b(n, block, before, then=None):
        seen = [start <= row_pos for start in starts_of(block)]
        k, v = keys_of(block), values_of(before)
        for h, cols in tiles:
            fade = fade_of(n - 1, h, cols)
            part_a(n % 2, h, cols, k, seen, None)
            part_b((n - 1) % 2, h, cols, v, fade)
            if then is not None:
                then(h, cols)

    own_group(0)
    starts = starts_of(my_block)
    inside = lax.broadcasted_iota(jnp.int32, (SPAN, ROWS), 0)
    masks = [inside + start <= row_pos for start in starts]
    own_keys = keys_of(my_block)
    for h, cols in tiles:
        part_a(0, h, cols, own_keys, [start <= row_pos for start in starts], masks)
    for i, (h, dy, c) in enumerate(relations):
        block = (((xh + h) & 1) * 4 + ((y + dy) & 3)) * 2 + ((core + c) & 1)
        arrived(posb.at[block], pos_recv.at[i])

    def two_blocks(j, carry):
        for g in range(7):
            @pl.when(j == g)
            def comm(g=g):
                own_group(g + 1)
                cross_group(g)
        a_beside_b(1, nth_block(j, 1), nth_block(j, 0))
        a_beside_b(2, nth_block(j + 1, 0), nth_block(j, 1))
        return carry

    lax.fori_loop(0, 7, two_blocks, 0)
    cross_group(7)
    last_values = values_of(nth_block(7, 1))

    def finish(h, cols):
        part_b(1, h, cols, last_values, fade_of(1, h, cols))
        scale = 1.0 / total[h, :, cols]
        done = (acc[h, :, cols] * scale).astype(bf16)
        for i in range(TILE // PART):
            t = cols.start // PART + i
            a_own[t, h * 128 : (h + 1) * 128, :] = done[:, i * PART : (i + 1) * PART]
            if h == 1:
                send(a_own.at[t], a_oth.at[t], a_send.at[t], a_recv.at[t], mate)

    a_beside_b(1, nth_block(7, 1), nth_block(7, 0), finish)

    weights_in(0)
    weights_crossed(0)

    def project(offset, t, rows=slice(None)):
        tile = ((z + offset) & 7) * 2 + xl
        return jnp.dot(wT[tile, rows], a_own[t], preferred_element_type=f32) + jnp.dot(
            w_oth[OFFSETS.index(offset), rows], a_oth[t], preferred_element_type=f32
        )

    def half_rows(d):
        return slice(d * 128, (d + 1) * 128)

    def send_half(d, half, t, sem):
        rows = pl.ds(half * 128, 128)
        send(z_out.at[d, 2, t, rows], z_in.at[d, 2, t, rows], z_send.at[d, sem, t], z_recv.at[d, sem, t],
             along[d])

    def up_and_down():
        return ((0, 1), (1, -1))

    def farthest(t, carry):
        arrived(a_oth.at[t], a_recv.at[t])
        part = project(4, t)
        for d, sign in up_and_down():
            z_out4[d, t] = part[half_rows(d)].astype(bf16)
            send(z_out4.at[d, t], z_in4.at[d, t], z_send.at[d, 3, t], z_recv.at[d, 3, t], along[d])
        for d, sign in up_and_down():
            z_out[d, 2, t, half_rows(1 - d), :] = project(sign * 3, t, half_rows(1 - d)).astype(bf16)
            send_half(d, 1 - d, t, 4)
        return carry

    def third(t, carry):
        for d, sign in up_and_down():
            part = project(sign * 3, t, half_rows(d))
            arrived(z_in4.at[d, t], z_recv.at[d, 3, t])
            z_out[d, 2, t, half_rows(d), :] = (part + z_in4[d, t].astype(f32)).astype(bf16)
            send_half(d, d, t, 2)
        return carry

    def nearer(k, t, carry):
        for d, sign in up_and_down():
            part = project(sign * k, t)
            if k == 2:
                arrived(z_in.at[d, 2, t, pl.ds((1 - d) * 128, 128)], z_recv.at[d, 4, t])
                arrived(z_in.at[d, 2, t, pl.ds(d * 128, 128)], z_recv.at[d, 2, t])
            else:
                arrived(z_in.at[d, k, t], z_recv.at[d, k, t])
            z_out[d, k - 1, t] = (part + z_in[d, k, t].astype(f32)).astype(bf16)
            send(z_out.at[d, k - 1, t], z_in.at[d, k - 1, t], z_send.at[d, k - 1, t],
                 z_recv.at[d, k - 1, t], along[d])
        return carry

    lax.fori_loop(0, PARTS, farthest, 0)
    weights_out(1)
    lax.fori_loop(0, PARTS, third, 0)
    weights_in(1)
    weights_crossed(1)
    lax.fori_loop(0, PARTS, functools.partial(nearer, 2), 0)
    lax.fori_loop(0, PARTS, functools.partial(nearer, 1), 0)
    for t in range(PARTS):
        part = project(0, t)
        for d in range(2):
            arrived(z_in.at[d, 0, t], z_recv.at[d, 0, t])
        out_ref[:, t * PART : (t + 1) * PART] = (
            part + (z_in[0, 0, t].astype(f32) + z_in[1, 0, t].astype(f32))
        ).astype(bf16)

    for i, (f, s, half) in enumerate(passed):
        sent_off(view_of(f, s, half), kv_send.at[i])
    for i in range(len(relations)):
        sent_off(posb.at[my_block], pos_send.at[i])
    for j in range(2):
        for side in range(2):
            for leg in range(2):
                sent_off(wT.at[0], w_send.at[j, side, leg])
    for t in range(PARTS):
        sent_off(a_own.at[t], a_send.at[t])
        for d in range(2):
            sent_off(z_out4.at[d, t], z_send.at[d, 3, t])
            for k in range(2):
                sent_off(z_out.at[d, k, t], z_send.at[d, k, t])
            for sem in (2, 4):
                sent_off(z_out4.at[d, t], z_send.at[d, sem, t])


def body(queries, keys, values, positions, out_weight):
    hbm = pl.BlockSpec(memory_space=pltpu.HBM)
    dma = pltpu.SemaphoreType.DMA
    return pl.pallas_call(
        kernel,
        out_shape=jax.ShapeDtypeStruct((256, ROWS), bf16),
        in_specs=[hbm] * 5,
        out_specs=pl.BlockSpec(memory_space=pltpu.VMEM),
        scratch_shapes=[
            pltpu.VMEM((ROWS, 256), bf16),
            pltpu.VMEM((1, ROWS), jnp.int32),
            pltpu.VMEM((16, 2, 128, ROWS), bf16),
            pltpu.VMEM((16, 1, 256), jnp.int32),
            pltpu.VMEM((2, 256, ROWS), bf16),
            pltpu.VMEM((2, 2, ROWS, ROWS), f32),
            pltpu.VMEM((2, 2, 1, ROWS), f32),
            pltpu.VMEM((2, 2, 2, 1, ROWS), f32),
            pltpu.VMEM((2, 1, ROWS), f32),
            pltpu.VMEM((2, 128, ROWS), f32),
            pltpu.VMEM((256, 4096), bf16),
            pltpu.VMEM((16, 256, 256), bf16),
            pltpu.VMEM((8, 256, 256), bf16),
            pltpu.VMEM((PARTS, 256, PART), bf16),
            pltpu.VMEM((PARTS, 256, PART), bf16),
            pltpu.VMEM((2, 3, PARTS, 256, PART), bf16),
            pltpu.VMEM((2, 3, PARTS, 256, PART), bf16),
            pltpu.VMEM((2, PARTS, 128, PART), bf16),
            pltpu.VMEM((2, PARTS, 128, PART), bf16),
            dma((5,)),
            dma((36,)),
            dma((4, 4, 2)),
            dma((4, 4)),
            dma((15,)),
            dma((15,)),
            dma((2, 2, 2)),
            dma((2, 2)),
            dma((2, 2)),
            dma((PARTS,)),
            dma((PARTS,)),
            dma((2, 5, PARTS)),
            dma((2, 5, PARTS)),
        ],
        compiler_params=pltpu.CompilerParams(
            collective_id=0, has_side_effects=True, vmem_limit_bytes=56 << 20
        ),
        cost_estimate=pl.CostEstimate(flops=6_000_000_000, bytes_accessed=4_000_000, transcendentals=8_400_000),
    )(queries, keys.T, values.T, positions.reshape(1, ROWS), out_weight)


def solution(mesh):
    in_specs = (P("ctx", "head"), P("ctx", "head"), P("ctx", "head"), P("ctx"), P("head", None))
    out_specs = P("head", "ctx")
    return jax.shard_map(body, mesh=mesh, in_specs=in_specs, out_specs=out_specs, check_vma=False)
```

```python
import functools

import jax
import jax.numpy as jnp
from jax import lax
from jax.experimental import pallas as pl
from jax.experimental.pallas import tpu as pltpu
from jax.sharding import PartitionSpec as P

SCALE = 0.08838834764831845
LOG2E = 1.4426950408889634
C = SCALE * LOG2E
NEG = -1e30
HIDE = 1e30
ROWS = 512
SPAN = 256
PARTS = 4
PART = ROWS // PARTS
TILE = 256
OFFSETS = (4, 3, -3, 2, -2, 1, -1, 0)
f32 = jnp.float32
bf16 = jnp.bfloat16
MESH = pl.DeviceIdType.MESH


def kernel(
    q_hbm, k_hbm, v_hbm, pos_hbm, w_hbm, out_ref,
    q_ref, pos_ref, kv, posb, qT, scores, top, shift, total, acc, w_own, wT, w_oth, a_own, a_oth,
    z_out, z_in, z_out4, z_in4,
    load_sem, kv_send, kv_recv, kv_cross, pos_send, pos_recv, w_send, w_recv, w_cross,
    a_send, a_recv, z_send, z_recv,
):
    ctx = lax.axis_index("ctx")
    head = lax.axis_index("head")
    core = ctx & 1
    y = (ctx >> 1) & 3
    xh = ctx >> 3
    z = head >> 1
    xl = head & 1
    x = xh * 2 + xl

    def device(dx, dy, dz, dcore):
        nx = (x + dx) & 3
        ny = (y + dy) & 3
        nz = (z + dz) & 7
        nc = (core + dcore) & 1
        return {"ctx": ((nx >> 1) * 4 + ny) * 2 + nc, "head": nz * 2 + (nx & 1)}

    firsts = {d: device(core * d, (1 - core) * d, 0, 0) for d in (-2, -1, 1, 2)}
    seconds = {d: device((1 - core) * d, core * d, 0, 0) for d in (-1, 1)}
    first = firsts.get
    second = seconds.get

    other_core = device(0, 0, 0, 1)
    mate = device(1 - 2 * xl, 0, 0, 0)
    along = (device(0, 0, 1, 0), device(0, 0, -1, 0))

    def piece_of(f, s, lane):
        own = core if lane == 0 else 1 - core
        px = (x + s + own * (f - s)) & 3
        py = (y + f + own * (s - f)) & 3
        return ((px >> 1) * 4 + py) * 2 + own, px & 1

    def remote(src, dst, send_sem, recv_sem, target):
        return pltpu.make_async_remote_copy(
            src_ref=src, dst_ref=dst, send_sem=send_sem, recv_sem=recv_sem,
            device_id=target, device_id_type=MESH,
        )

    def send(src, dst, send_sem, recv_sem, target):
        remote(src, dst, send_sem, recv_sem, target).start()

    def sent_off(src, send_sem):
        remote(src, src, send_sem, load_sem.at[0], other_core).wait_send()

    def arrived(dst, recv_sem):
        remote(dst, dst, load_sem.at[0], recv_sem, other_core).wait_recv()

    loads = []

    def load(src, dst):
        copy = pltpu.make_async_copy(src, dst, load_sem.at[len(loads)])
        copy.start()
        loads.append(copy)

    my_block = ctx
    load(k_hbm, kv.at[my_block, xl, pl.ds(0, 64)])
    load(v_hbm, kv.at[my_block, xl, pl.ds(64, 64)])
    load(pos_hbm, pos_ref)
    load(q_hbm, q_ref)
    load(w_hbm, w_own)

    barrier = pltpu.get_barrier_semaphore()
    relations = [
        (h, dy, c) for h in range(2) for dy in range(4) for c in range(2) if (h, dy, c) != (0, 0, 0)
    ]
    friends = [device(2 * h, dy, 0, c) for h, dy, c in relations]
    friends += [device(1, 0, 0, 0), device(-1, 0, 0, 0), device(0, 0, 1, 0), device(0, 0, -1, 0)]
    for friend in friends:
        pl.semaphore_signal(barrier, inc=1, device_id=friend, device_id_type=MESH)
    for i in range(3):
        loads[i].wait()
    lane = lax.broadcasted_iota(jnp.int32, (1, 128), 1)
    posb[my_block, :, 0:128] = pos_ref[:, 0:128] - lane
    posb[my_block, :, 128:256] = pos_ref[:, SPAN : SPAN + 128] - lane
    pl.semaphore_wait(barrier, len(friends))

    passed = []

    def view_of(f, s, half):
        block, side = piece_of(f, s, 0)
        return kv.at[block, side] if half is None else kv.at[block, side, pl.ds(64 * half, 64)]

    def pass_on(f, s, target, f_there, s_there, half=None):
        view = view_of(f, s, half)
        send(view, view, kv_send.at[len(passed)],
             kv_recv.at[f_there % 4, s_there % 4, 0 if half is None else half], target)
        passed.append((f, s, half))

    def cross(f, s):
        view = view_of(f, s, None)
        send(view, view, kv_send.at[len(passed)], kv_cross.at[f, s], other_core)
        passed.append((f, s, None))

    def to_second(f):
        pass_on(f, 0, second(1), f, -1)
        pass_on(f, 0, second(-1), f, 1)

    def wait_piece(f, s):
        block, side = piece_of(f, s, 0)
        if s == 2 or (f, s) == (2, 0):
            for half in range(2):
                arrived(kv.at[block, side, pl.ds(64 * half, 64)], kv_recv.at[f, s, half])
        else:
            arrived(kv.at[block, side], kv_recv.at[f, s, 0])
        if s == 0:
            to_second(f)
        elif s == 3:
            pass_on(f, s, second(1), f, 2, half=0)
        elif s == 1:
            pass_on(f, s, second(-1), f, 2, half=1)
        cross(f, s)

    def wait_cross(f, s):
        block, side = piece_of(f, s, 1)
        arrived(kv.at[block, side], kv_cross.at[f, s])

    pass_on(0, 0, first(1), -1, 0)
    pass_on(0, 0, first(-1), 1, 0)
    pass_on(0, 0, first(2), 2, 0, half=0)
    pass_on(0, 0, first(-2), 2, 0, half=1)
    to_second(0)
    cross(0, 0)
    for i, (h, dy, c) in enumerate(relations):
        there = relations.index((h, (4 - dy) % 4, c))
        send(posb.at[my_block], posb.at[my_block], pos_send.at[i], pos_recv.at[there],
             device(2 * h, dy, 0, c))

    def weights_out(j):
        for side, d in ((0, 1), (1, -1)):
            slot = 4 * j + 2 * side + core
            offset = sum(
                (jnp.where(slot == i, o, 0) for i, o in enumerate(OFFSETS)), jnp.int32(0)
            )
            tile = ((z + offset) & 7) * 2 + 1 - xl
            send(wT.at[tile], w_oth.at[slot], w_send.at[j, side, 0], w_recv.at[j, side],
                 device(d, 0, 0, 0))

    def weights_in(j):
        for side in range(2):
            slot = 4 * j + 2 * side + core
            arrived(w_oth.at[slot], w_recv.at[j, side])
            send(w_oth.at[slot], w_oth.at[slot], w_send.at[j, side, 1], w_cross.at[j, side], other_core)

    def weights_crossed(j):
        for side in range(2):
            arrived(w_oth.at[4 * j + 2 * side + 1 - core], w_cross.at[j, side])

    loads[4].wait()
    for tile in range(16):
        wT[tile] = w_own[:, tile * 256 : (tile + 1) * 256].T
    loads[3].wait()
    for h in range(2):
        t = q_ref[:, h * 128 : (h + 1) * 128].T
        gap = jnp.zeros((64, ROWS), bf16)
        qT[h] = jnp.concatenate([t[:64], gap, t[64:], gap], axis=0)
    top[...] = jnp.full(top.shape, NEG, f32)
    total[...] = jnp.zeros(total.shape, f32)
    acc[...] = jnp.zeros(acc.shape, f32)

    row_pos = pos_ref[...]

    def starts_of(block):
        return [
            jnp.concatenate([posb[block, :, j * 128 : (j + 1) * 128]] * 4, axis=1) for j in range(2)
        ]

    def part_a(par, h, cols, k, seen, masks):
        s = jnp.dot(k, qT[h, :, cols], preferred_element_type=f32)
        if masks is not None:
            s = jnp.concatenate(
                [jnp.where(masks[j][:, cols], s[j * SPAN : (j + 1) * SPAN], NEG) for j in range(2)], axis=0
            )
        scores[par, h, :, cols] = s
        new = top[par, h, :, cols]
        for j in range(2):
            most = jnp.max(s[j * SPAN : (j + 1) * SPAN], axis=0, keepdims=True)
            new = jnp.maximum(new, jnp.where(seen[j][:, cols], most, NEG))
        top[1 - par, h, :, cols] = new
        for j in range(2):
            shift[par, h, j, :, cols] = new * C + jnp.where(seen[j][:, cols], 0.0, HIDE)

    def part_b(par, h, cols, v, fade):
        expo = [
            jnp.exp2(scores[par, h, j * SPAN : (j + 1) * SPAN, cols] * C - shift[par, h, j, :, cols])
            for j in range(2)
        ]
        total[h, :, cols] = total[h, :, cols] * fade + (
            jnp.sum(expo[0], axis=0, keepdims=True) + jnp.sum(expo[1], axis=0, keepdims=True)
        )
        more = jnp.dot(v, jnp.concatenate(expo, axis=0).astype(bf16), preferred_element_type=f32)
        acc[h, :, cols] = acc[h, :, cols] * fade + more

    tiles = [(h, slice(r * TILE, (r + 1) * TILE)) for r in range(ROWS // TILE) for h in range(2)]

    def keys_of(block):
        return jnp.concatenate([kv[block, 0], kv[block, 1]], axis=0).T

    def values_of(block):
        return jnp.concatenate([kv[block, 0, 64:], kv[block, 1, 64:]], axis=0)

    def fade_of(n, h, cols):
        par = n % 2
        return jnp.exp2((top[par, h, :, cols] - top[1 - par, h, :, cols]) * C)

    groups = (
        ((1, 0), (3, 0), (2, 0), (0, 1), (0, 3)),
        ((1, 1), (1, 3)),
        ((3, 1), (3, 3)),
        ((2, 1), (2, 3)),
        ((0, 2),),
        ((1, 2),),
        ((3, 2),),
        ((2, 2),),
    )
    orders = ((0, 1, 3, 2, 4, 5, 7, 6), (0, 4, 1, 3, 5, 7, 2, 6))

    coded = [sum(code << (3 * i) for i, code in enumerate(order)) for order in orders]

    def nth_block(n, which):
        number = core if which == 0 else 1 - core
        code = ((coded[0] + number * (coded[1] - coded[0])) >> (3 * n)) & 7
        return ((((xh + (code >> 2)) & 1) * 4) + ((y + code) & 3)) * 2 + number

    def own_group(g):
        for f, s in groups[g]:
            wait_piece(f, s)
        if g == 3:
            weights_out(0)
        if g == 5:
            weights_out(1)

    def cross_group(g):
        for f, s in (((0, 0),) if g == 0 else ()) + groups[g]:
            wait_cross(f, s)

    def a_beside_b(n, block, before, then=None):
        seen = [start <= row_pos for start in starts_of(block)]
        k, v = keys_of(block), values_of(before)
        for h, cols in tiles:
            fade = fade_of(n - 1, h, cols)
            part_a(n % 2, h, cols, k, seen, None)
            part_b((n - 1) % 2, h, cols, v, fade)
            if then is not None:
                then(h, cols)

    own_group(0)
    starts = starts_of(my_block)
    inside = lax.broadcasted_iota(jnp.int32, (SPAN, ROWS), 0)
    masks = [inside + start <= row_pos for start in starts]
    own_keys = keys_of(my_block)
    for h, cols in tiles:
        part_a(0, h, cols, own_keys, [start <= row_pos for start in starts], masks)
    for i, (h, dy, c) in enumerate(relations):
        block = (((xh + h) & 1) * 4 + ((y + dy) & 3)) * 2 + ((core + c) & 1)
        arrived(posb.at[block], pos_recv.at[i])

    def two_blocks(j, carry):
        for g in range(7):
            @pl.when(j == g)
            def comm(g=g):
                own_group(g + 1)
                cross_group(g)
        a_beside_b(1, nth_block(j, 1), nth_block(j, 0))
        a_beside_b(2, nth_block(j + 1, 0), nth_block(j, 1))
        return carry

    lax.fori_loop(0, 7, two_blocks, 0)
    cross_group(7)
    weights_in(0)
    last_values = values_of(nth_block(7, 1))

    def finish(h, cols):
        part_b(1, h, cols, last_values, fade_of(1, h, cols))
        scale = 1.0 / total[h, :, cols]
        done = (acc[h, :, cols] * scale).astype(bf16)
        for i in range(TILE // PART):
            t = cols.start // PART + i
            a_own[t, h * 128 : (h + 1) * 128, :] = done[:, i * PART : (i + 1) * PART]
            if h == 1:
                send(a_own.at[t], a_oth.at[t], a_send.at[t], a_recv.at[t], mate)

    a_beside_b(1, nth_block(7, 1), nth_block(7, 0), finish)

    weights_crossed(0)

    def project(offset, t, rows=slice(None)):
        tile = ((z + offset) & 7) * 2 + xl
        return jnp.dot(wT[tile, rows], a_own[t], preferred_element_type=f32) + jnp.dot(
            w_oth[OFFSETS.index(offset), rows], a_oth[t], preferred_element_type=f32
        )

    def half_rows(d):
        return slice(d * 128, (d + 1) * 128)

    def send_half(d, half, t, sem):
        rows = pl.ds(half * 128, 128)
        send(z_out.at[d, 2, t, rows], z_in.at[d, 2, t, rows], z_send.at[d, sem, t], z_recv.at[d, sem, t],
             along[d])

    def up_and_down():
        return ((0, 1), (1, -1))

    def farthest(t, carry):
        arrived(a_oth.at[t], a_recv.at[t])
        part = project(4, t)
        for d, sign in up_and_down():
            z_out4[d, t] = part[half_rows(d)].astype(bf16)
            send(z_out4.at[d, t], z_in4.at[d, t], z_send.at[d, 3, t], z_recv.at[d, 3, t], along[d])
        for d, sign in up_and_down():
            z_out[d, 2, t, half_rows(1 - d), :] = project(sign * 3, t, half_rows(1 - d)).astype(bf16)
            send_half(d, 1 - d, t, 4)
        return carry

    def third(t, carry):
        for d, sign in up_and_down():
            part = project(sign * 3, t, half_rows(d))
            arrived(z_in4.at[d, t], z_recv.at[d, 3, t])
            z_out[d, 2, t, half_rows(d), :] = (part + z_in4[d, t].astype(f32)).astype(bf16)
            send_half(d, d, t, 2)
        return carry

    def nearer(k, t, carry):
        for d, sign in up_and_down():
            part = project(sign * k, t)
            if k == 2:
                arrived(z_in.at[d, 2, t, pl.ds((1 - d) * 128, 128)], z_recv.at[d, 4, t])
                arrived(z_in.at[d, 2, t, pl.ds(d * 128, 128)], z_recv.at[d, 2, t])
            else:
                arrived(z_in.at[d, k, t], z_recv.at[d, k, t])
            z_out[d, k - 1, t] = (part + z_in[d, k, t].astype(f32)).astype(bf16)
            send(z_out.at[d, k - 1, t], z_in.at[d, k - 1, t], z_send.at[d, k - 1, t],
                 z_recv.at[d, k - 1, t], along[d])
        return carry

    lax.fori_loop(0, PARTS, farthest, 0)
    weights_in(1)
    lax.fori_loop(0, PARTS, third, 0)
    weights_crossed(1)
    lax.fori_loop(0, PARTS, functools.partial(nearer, 2), 0)
    lax.fori_loop(0, PARTS, functools.partial(nearer, 1), 0)
    for t in range(PARTS):
        part = project(0, t)
        for d in range(2):
            arrived(z_in.at[d, 0, t], z_recv.at[d, 0, t])
        out_ref[:, t * PART : (t + 1) * PART] = (
            part + (z_in[0, 0, t].astype(f32) + z_in[1, 0, t].astype(f32))
        ).astype(bf16)

    for i, (f, s, half) in enumerate(passed):
        sent_off(view_of(f, s, half), kv_send.at[i])
    for i in range(len(relations)):
        sent_off(posb.at[my_block], pos_send.at[i])
    for j in range(2):
        for side in range(2):
            for leg in range(2):
                sent_off(wT.at[0], w_send.at[j, side, leg])
    for t in range(PARTS):
        sent_off(a_own.at[t], a_send.at[t])
        for d in range(2):
            sent_off(z_out4.at[d, t], z_send.at[d, 3, t])
            for k in range(2):
                sent_off(z_out.at[d, k, t], z_send.at[d, k, t])
            for sem in (2, 4):
                sent_off(z_out4.at[d, t], z_send.at[d, sem, t])


def body(queries, keys, values, positions, out_weight):
    hbm = pl.BlockSpec(memory_space=pltpu.HBM)
    dma = pltpu.SemaphoreType.DMA
    return pl.pallas_call(
        kernel,
        out_shape=jax.ShapeDtypeStruct((256, ROWS), bf16),
        in_specs=[hbm] * 5,
        out_specs=pl.BlockSpec(memory_space=pltpu.VMEM),
        scratch_shapes=[
            pltpu.VMEM((ROWS, 256), bf16),
            pltpu.VMEM((1, ROWS), jnp.int32),
            pltpu.VMEM((16, 2, 128, ROWS), bf16),
            pltpu.VMEM((16, 1, 256), jnp.int32),
            pltpu.VMEM((2, 256, ROWS), bf16),
            pltpu.VMEM((2, 2, ROWS, ROWS), f32),
            pltpu.VMEM((2, 2, 1, ROWS), f32),
            pltpu.VMEM((2, 2, 2, 1, ROWS), f32),
            pltpu.VMEM((2, 1, ROWS), f32),
            pltpu.VMEM((2, 128, ROWS), f32),
            pltpu.VMEM((256, 4096), bf16),
            pltpu.VMEM((16, 256, 256), bf16),
            pltpu.VMEM((8, 256, 256), bf16),
            pltpu.VMEM((PARTS, 256, PART), bf16),
            pltpu.VMEM((PARTS, 256, PART), bf16),
            pltpu.VMEM((2, 3, PARTS, 256, PART), bf16),
            pltpu.VMEM((2, 3, PARTS, 256, PART), bf16),
            pltpu.VMEM((2, PARTS, 128, PART), bf16),
            pltpu.VMEM((2, PARTS, 128, PART), bf16),
            dma((5,)),
            dma((36,)),
            dma((4, 4, 2)),
            dma((4, 4)),
            dma((15,)),
            dma((15,)),
            dma((2, 2, 2)),
            dma((2, 2)),
            dma((2, 2)),
            dma((PARTS,)),
            dma((PARTS,)),
            dma((2, 5, PARTS)),
            dma((2, 5, PARTS)),
        ],
        compiler_params=pltpu.CompilerParams(
            collective_id=0, has_side_effects=True, vmem_limit_bytes=56 << 20
        ),
        cost_estimate=pl.CostEstimate(flops=6_000_000_000, bytes_accessed=4_000_000, transcendentals=8_400_000),
    )(queries, keys.T, values.T, positions.reshape(1, ROWS), out_weight)


def solution(mesh):
    in_specs = (P("ctx", "head"), P("ctx", "head"), P("ctx", "head"), P("ctx"), P("head", None))
    out_specs = P("head", "ctx")
    return jax.shard_map(body, mesh=mesh, in_specs=in_specs, out_specs=out_specs, check_vma=False)
```

```python
import functools

import jax
import jax.numpy as jnp
from jax import lax
from jax.experimental import pallas as pl
from jax.experimental.pallas import tpu as pltpu
from jax.sharding import PartitionSpec as P

SCALE = 0.08838834764831845
LOG2E = 1.4426950408889634
C = SCALE * LOG2E
NEG = -1e30
HIDE = 1e30
ROWS = 512
SPAN = 256
PARTS = 4
PART = ROWS // PARTS
TILE = 256
BOTH = (2,)
OFFSETS = (4, 3, -3, 2, -2, 1, -1, 0)
f32 = jnp.float32
bf16 = jnp.bfloat16
MESH = pl.DeviceIdType.MESH


def kernel(
    q_hbm, k_hbm, v_hbm, pos_hbm, w_hbm, out_ref,
    q_ref, pos_ref, kv, posb, qT, scores, top, shift, total, acc, w_own, wT, w_oth, a_own, a_oth,
    z_out, z_in, z_out4, z_in4,
    load_sem, kv_send, kv_recv, kv_cross, pos_send, pos_recv, w_send, w_recv, w_cross,
    a_send, a_recv, z_send, z_recv,
):
    ctx = lax.axis_index("ctx")
    head = lax.axis_index("head")
    core = ctx & 1
    y = (ctx >> 1) & 3
    xh = ctx >> 3
    z = head >> 1
    xl = head & 1
    x = xh * 2 + xl

    def device(dx, dy, dz, dcore):
        nx = (x + dx) & 3
        ny = (y + dy) & 3
        nz = (z + dz) & 7
        nc = (core + dcore) & 1
        return {"ctx": ((nx >> 1) * 4 + ny) * 2 + nc, "head": nz * 2 + (nx & 1)}

    firsts = {d: device(core * d, (1 - core) * d, 0, 0) for d in (-2, -1, 1, 2)}
    second_other = {d: device((1 - core) * d, core * d, 0, 1) for d in (-1, 1)}.get
    seconds = {d: device((1 - core) * d, core * d, 0, 0) for d in (-1, 1)}
    first = firsts.get
    second = seconds.get

    other_core = device(0, 0, 0, 1)
    mate = device(1 - 2 * xl, 0, 0, 0)
    along = (device(0, 0, 1, 0), device(0, 0, -1, 0))

    def piece_of(f, s, lane):
        own = core if lane == 0 else 1 - core
        px = (x + s + own * (f - s)) & 3
        py = (y + f + own * (s - f)) & 3
        return ((px >> 1) * 4 + py) * 2 + own, px & 1

    def remote(src, dst, send_sem, recv_sem, target):
        return pltpu.make_async_remote_copy(
            src_ref=src, dst_ref=dst, send_sem=send_sem, recv_sem=recv_sem,
            device_id=target, device_id_type=MESH,
        )

    def send(src, dst, send_sem, recv_sem, target):
        remote(src, dst, send_sem, recv_sem, target).start()

    def sent_off(src, send_sem):
        remote(src, src, send_sem, load_sem.at[0], other_core).wait_send()

    def arrived(dst, recv_sem):
        remote(dst, dst, load_sem.at[0], recv_sem, other_core).wait_recv()

    loads = []

    def load(src, dst):
        copy = pltpu.make_async_copy(src, dst, load_sem.at[len(loads)])
        copy.start()
        loads.append(copy)

    my_block = ctx
    load(k_hbm, kv.at[my_block, xl, pl.ds(0, 64)])
    load(v_hbm, kv.at[my_block, xl, pl.ds(64, 64)])
    load(pos_hbm, pos_ref)
    load(q_hbm, q_ref)
    load(w_hbm, w_own)

    barrier = pltpu.get_barrier_semaphore()
    relations = [
        (h, dy, c) for h in range(2) for dy in range(4) for c in range(2) if (h, dy, c) != (0, 0, 0)
    ]
    friends = [device(2 * h, dy, 0, c) for h, dy, c in relations]
    friends += [device(1, 0, 0, 0), device(-1, 0, 0, 0), device(0, 0, 1, 0), device(0, 0, -1, 0)]
    friends += [device(1, 0, 0, 1), device(-1, 0, 0, 1)]
    for friend in friends:
        pl.semaphore_signal(barrier, inc=1, device_id=friend, device_id_type=MESH)
    for i in range(3):
        loads[i].wait()
    lane = lax.broadcasted_iota(jnp.int32, (1, 128), 1)
    posb[my_block, :, 0:128] = pos_ref[:, 0:128] - lane
    posb[my_block, :, 128:256] = pos_ref[:, SPAN : SPAN + 128] - lane
    pl.semaphore_wait(barrier, len(friends))

    passed = []

    def view_of(f, s, half):
        block, side = piece_of(f, s, 0)
        return kv.at[block, side] if half is None else kv.at[block, side, pl.ds(64 * half, 64)]

    def pass_on(f, s, target, f_there, s_there, half=None):
        view = view_of(f, s, half)
        send(view, view, kv_send.at[len(passed)],
             kv_recv.at[f_there % 4, s_there % 4, 0 if half is None else half], target)
        passed.append((f, s, half))

    def cross(f, s):
        view = view_of(f, s, None)
        send(view, view, kv_send.at[len(passed)], kv_cross.at[f, s], other_core)
        passed.append((f, s, None))

    def to_other(f, s, target, half):
        view = view_of(f, s, half)
        send(view, view, kv_send.at[len(passed)], kv_cross.at[f, 2], target)
        passed.append((f, s, half))

    def to_second(f):
        pass_on(f, 0, second(1), f, -1)
        pass_on(f, 0, second(-1), f, 1)

    def wait_piece(f, s):
        block, side = piece_of(f, s, 0)
        if s == 2 or (f, s) == (2, 0):
            for half in range(2):
                arrived(kv.at[block, side, pl.ds(64 * half, 64)], kv_recv.at[f, s, half])
        else:
            arrived(kv.at[block, side], kv_recv.at[f, s, 0])
        if s == 0:
            to_second(f)
        elif s == 3:
            pass_on(f, s, second(1), f, 2, half=0)
            if f in BOTH:
                to_other(f, s, second_other(1), half=0)
        elif s == 1:
            pass_on(f, s, second(-1), f, 2, half=1)
            if f in BOTH:
                to_other(f, s, second_other(-1), half=1)
        if s != 2 or f not in BOTH:
            cross(f, s)

    def wait_cross(f, s):
        block, side = piece_of(f, s, 1)
        arrived(kv.at[block, side], kv_cross.at[f, s])

    pass_on(0, 0, first(1), -1, 0)
    pass_on(0, 0, first(-1), 1, 0)
    pass_on(0, 0, first(2), 2, 0, half=0)
    pass_on(0, 0, first(-2), 2, 0, half=1)
    to_second(0)
    cross(0, 0)
    for i, (h, dy, c) in enumerate(relations):
        there = relations.index((h, (4 - dy) % 4, c))
        send(posb.at[my_block], posb.at[my_block], pos_send.at[i], pos_recv.at[there],
             device(2 * h, dy, 0, c))

    def weights_out(j):
        for side, d in ((0, 1), (1, -1)):
            slot = 4 * j + 2 * side + core
            offset = sum(
                (jnp.where(slot == i, o, 0) for i, o in enumerate(OFFSETS)), jnp.int32(0)
            )
            tile = ((z + offset) & 7) * 2 + 1 - xl
            send(wT.at[tile], w_oth.at[slot], w_send.at[j, side, 0], w_recv.at[j, side],
                 device(d, 0, 0, 0))

    def weights_in(j):
        for side in range(2):
            slot = 4 * j + 2 * side + core
            arrived(w_oth.at[slot], w_recv.at[j, side])
            send(w_oth.at[slot], w_oth.at[slot], w_send.at[j, side, 1], w_cross.at[j, side], other_core)

    def weights_crossed(j):
        for side in range(2):
            arrived(w_oth.at[4 * j + 2 * side + 1 - core], w_cross.at[j, side])

    loads[4].wait()
    for tile in range(16):
        wT[tile] = w_own[:, tile * 256 : (tile + 1) * 256].T
    loads[3].wait()
    for h in range(2):
        t = q_ref[:, h * 128 : (h + 1) * 128].T
        gap = jnp.zeros((64, ROWS), bf16)
        qT[h] = jnp.concatenate([t[:64], gap, t[64:], gap], axis=0)
    top[...] = jnp.full(top.shape, NEG, f32)
    total[...] = jnp.zeros(total.shape, f32)
    acc[...] = jnp.zeros(acc.shape, f32)

    row_pos = pos_ref[...]

    def starts_of(block):
        return [
            jnp.concatenate([posb[block, :, j * 128 : (j + 1) * 128]] * 4, axis=1) for j in range(2)
        ]

    def part_a(par, h, cols, k, seen, masks):
        s = jnp.dot(k, qT[h, :, cols], preferred_element_type=f32)
        if masks is not None:
            s = jnp.concatenate(
                [jnp.where(masks[j][:, cols], s[j * SPAN : (j + 1) * SPAN], NEG) for j in range(2)], axis=0
            )
        scores[par, h, :, cols] = s
        new = top[par, h, :, cols]
        for j in range(2):
            most = jnp.max(s[j * SPAN : (j + 1) * SPAN], axis=0, keepdims=True)
            new = jnp.maximum(new, jnp.where(seen[j][:, cols], most, NEG))
        top[1 - par, h, :, cols] = new
        for j in range(2):
            shift[par, h, j, :, cols] = new * C + jnp.where(seen[j][:, cols], 0.0, HIDE)

    def part_b(par, h, cols, v, fade):
        expo = [
            jnp.exp2(scores[par, h, j * SPAN : (j + 1) * SPAN, cols] * C - shift[par, h, j, :, cols])
            for j in range(2)
        ]
        total[h, :, cols] = total[h, :, cols] * fade + (
            jnp.sum(expo[0], axis=0, keepdims=True) + jnp.sum(expo[1], axis=0, keepdims=True)
        )
        more = jnp.dot(v, jnp.concatenate(expo, axis=0).astype(bf16), preferred_element_type=f32)
        acc[h, :, cols] = acc[h, :, cols] * fade + more

    tiles = [(h, slice(r * TILE, (r + 1) * TILE)) for r in range(ROWS // TILE) for h in range(2)]

    def keys_of(block):
        return jnp.concatenate([kv[block, 0], kv[block, 1]], axis=0).T

    def values_of(block):
        return jnp.concatenate([kv[block, 0, 64:], kv[block, 1, 64:]], axis=0)

    def fade_of(n, h, cols):
        par = n % 2
        return jnp.exp2((top[par, h, :, cols] - top[1 - par, h, :, cols]) * C)

    groups = (
        ((1, 0), (3, 0), (2, 0), (0, 1), (0, 3)),
        ((1, 1), (1, 3)),
        ((3, 1), (3, 3)),
        ((2, 1), (2, 3)),
        ((0, 2),),
        ((1, 2),),
        ((3, 2),),
        ((2, 2),),
    )
    orders = ((0, 1, 3, 2, 4, 5, 7, 6), (0, 4, 1, 3, 5, 7, 2, 6))

    coded = [sum(code << (3 * i) for i, code in enumerate(order)) for order in orders]

    def nth_block(n, which):
        number = core if which == 0 else 1 - core
        code = ((coded[0] + number * (coded[1] - coded[0])) >> (3 * n)) & 7
        return ((((xh + (code >> 2)) & 1) * 4) + ((y + code) & 3)) * 2 + number

    def own_group(g):
        for f, s in groups[g]:
            wait_piece(f, s)
        if g == 3:
            weights_out(0)
        if g == 5:
            weights_out(1)

    def cross_group(g):
        for f, s in (((0, 0),) if g == 0 else ()) + groups[g]:
            wait_cross(f, s)

    def a_beside_b(n, block, before, then=None):
        seen = [start <= row_pos for start in starts_of(block)]
        k, v = keys_of(block), values_of(before)
        for h, cols in tiles:
            fade = fade_of(n - 1, h, cols)
            part_a(n % 2, h, cols, k, seen, None)
            part_b((n - 1) % 2, h, cols, v, fade)
            if then is not None:
                then(h, cols)

    own_group(0)
    starts = starts_of(my_block)
    inside = lax.broadcasted_iota(jnp.int32, (SPAN, ROWS), 0)
    masks = [inside + start <= row_pos for start in starts]
    own_keys = keys_of(my_block)
    for h, cols in tiles:
        part_a(0, h, cols, own_keys, [start <= row_pos for start in starts], masks)
    for i, (h, dy, c) in enumerate(relations):
        block = (((xh + h) & 1) * 4 + ((y + dy) & 3)) * 2 + ((core + c) & 1)
        arrived(posb.at[block], pos_recv.at[i])

    def two_blocks(j, carry):
        for g in range(7):
            @pl.when(j == g)
            def comm(g=g):
                own_group(g + 1)
                cross_group(g)
        a_beside_b(1, nth_block(j, 1), nth_block(j, 0))
        a_beside_b(2, nth_block(j + 1, 0), nth_block(j, 1))
        return carry

    lax.fori_loop(0, 7, two_blocks, 0)
    cross_group(7)
    weights_in(0)
    last_values = values_of(nth_block(7, 1))

    def finish(h, cols):
        part_b(1, h, cols, last_values, fade_of(1, h, cols))
        scale = 1.0 / total[h, :, cols]
        done = (acc[h, :, cols] * scale).astype(bf16)
        for i in range(TILE // PART):
            t = cols.start // PART + i
            a_own[t, h * 128 : (h + 1) * 128, :] = done[:, i * PART : (i + 1) * PART]
            if h == 1:
                send(a_own.at[t], a_oth.at[t], a_send.at[t], a_recv.at[t], mate)

    a_beside_b(1, nth_block(7, 1), nth_block(7, 0), finish)

    weights_crossed(0)

    def project(offset, t, rows=slice(None)):
        tile = ((z + offset) & 7) * 2 + xl
        return jnp.dot(wT[tile, rows], a_own[t], preferred_element_type=f32) + jnp.dot(
            w_oth[OFFSETS.index(offset), rows], a_oth[t], preferred_element_type=f32
        )

    def half_rows(d):
        return slice(d * 128, (d + 1) * 128)

    def send_half(d, half, t, sem):
        rows = pl.ds(half * 128, 128)
        send(z_out.at[d, 2, t, rows], z_in.at[d, 2, t, rows], z_send.at[d, sem, t], z_recv.at[d, sem, t],
             along[d])

    def up_and_down():
        return ((0, 1), (1, -1))

    def farthest(t, carry):
        arrived(a_oth.at[t], a_recv.at[t])
        part = project(4, t)
        for d, sign in up_and_down():
            z_out4[d, t] = part[half_rows(d)].astype(bf16)
            send(z_out4.at[d, t], z_in4.at[d, t], z_send.at[d, 3, t], z_recv.at[d, 3, t], along[d])
        for d, sign in up_and_down():
            z_out[d, 2, t, half_rows(1 - d), :] = project(sign * 3, t, half_rows(1 - d)).astype(bf16)
            send_half(d, 1 - d, t, 4)
        return carry

    def third(t, carry):
        for d, sign in up_and_down():
            part = project(sign * 3, t, half_rows(d))
            arrived(z_in4.at[d, t], z_recv.at[d, 3, t])
            z_out[d, 2, t, half_rows(d), :] = (part + z_in4[d, t].astype(f32)).astype(bf16)
            send_half(d, d, t, 2)
        return carry

    def nearer(k, t, carry):
        for d, sign in up_and_down():
            part = project(sign * k, t)
            if k == 2:
                arrived(z_in.at[d, 2, t, pl.ds((1 - d) * 128, 128)], z_recv.at[d, 4, t])
                arrived(z_in.at[d, 2, t, pl.ds(d * 128, 128)], z_recv.at[d, 2, t])
            else:
                arrived(z_in.at[d, k, t], z_recv.at[d, k, t])
            z_out[d, k - 1, t] = (part + z_in[d, k, t].astype(f32)).astype(bf16)
            send(z_out.at[d, k - 1, t], z_in.at[d, k - 1, t], z_send.at[d, k - 1, t],
                 z_recv.at[d, k - 1, t], along[d])
        return carry

    lax.fori_loop(0, PARTS, farthest, 0)
    weights_in(1)
    lax.fori_loop(0, PARTS, third, 0)
    weights_crossed(1)
    lax.fori_loop(0, PARTS, functools.partial(nearer, 2), 0)
    lax.fori_loop(0, PARTS, functools.partial(nearer, 1), 0)
    for t in range(PARTS):
        part = project(0, t)
        for d in range(2):
            arrived(z_in.at[d, 0, t], z_recv.at[d, 0, t])
        out_ref[:, t * PART : (t + 1) * PART] = (
            part + (z_in[0, 0, t].astype(f32) + z_in[1, 0, t].astype(f32))
        ).astype(bf16)

    for i, (f, s, half) in enumerate(passed):
        sent_off(view_of(f, s, half), kv_send.at[i])
    for i in range(len(relations)):
        sent_off(posb.at[my_block], pos_send.at[i])
    for j in range(2):
        for side in range(2):
            for leg in range(2):
                sent_off(wT.at[0], w_send.at[j, side, leg])
    for t in range(PARTS):
        sent_off(a_own.at[t], a_send.at[t])
        for d in range(2):
            sent_off(z_out4.at[d, t], z_send.at[d, 3, t])
            for k in range(2):
                sent_off(z_out.at[d, k, t], z_send.at[d, k, t])
            for sem in (2, 4):
                sent_off(z_out4.at[d, t], z_send.at[d, sem, t])


def body(queries, keys, values, positions, out_weight):
    hbm = pl.BlockSpec(memory_space=pltpu.HBM)
    dma = pltpu.SemaphoreType.DMA
    return pl.pallas_call(
        kernel,
        out_shape=jax.ShapeDtypeStruct((256, ROWS), bf16),
        in_specs=[hbm] * 5,
        out_specs=pl.BlockSpec(memory_space=pltpu.VMEM),
        scratch_shapes=[
            pltpu.VMEM((ROWS, 256), bf16),
            pltpu.VMEM((1, ROWS), jnp.int32),
            pltpu.VMEM((16, 2, 128, ROWS), bf16),
            pltpu.VMEM((16, 1, 256), jnp.int32),
            pltpu.VMEM((2, 256, ROWS), bf16),
            pltpu.VMEM((2, 2, ROWS, ROWS), f32),
            pltpu.VMEM((2, 2, 1, ROWS), f32),
            pltpu.VMEM((2, 2, 2, 1, ROWS), f32),
            pltpu.VMEM((2, 1, ROWS), f32),
            pltpu.VMEM((2, 128, ROWS), f32),
            pltpu.VMEM((256, 4096), bf16),
            pltpu.VMEM((16, 256, 256), bf16),
            pltpu.VMEM((8, 256, 256), bf16),
            pltpu.VMEM((PARTS, 256, PART), bf16),
            pltpu.VMEM((PARTS, 256, PART), bf16),
            pltpu.VMEM((2, 3, PARTS, 256, PART), bf16),
            pltpu.VMEM((2, 3, PARTS, 256, PART), bf16),
            pltpu.VMEM((2, PARTS, 128, PART), bf16),
            pltpu.VMEM((2, PARTS, 128, PART), bf16),
            dma((5,)),
            dma((36 + len(BOTH),)),
            dma((4, 4, 2)),
            dma((4, 4)),
            dma((15,)),
            dma((15,)),
            dma((2, 2, 2)),
            dma((2, 2)),
            dma((2, 2)),
            dma((PARTS,)),
            dma((PARTS,)),
            dma((2, 5, PARTS)),
            dma((2, 5, PARTS)),
        ],
        compiler_params=pltpu.CompilerParams(
            collective_id=0, has_side_effects=True, vmem_limit_bytes=56 << 20
        ),
        cost_estimate=pl.CostEstimate(flops=6_000_000_000, bytes_accessed=4_000_000, transcendentals=8_400_000),
    )(queries, keys.T, values.T, positions.reshape(1, ROWS), out_weight)


def solution(mesh):
    in_specs = (P("ctx", "head"), P("ctx", "head"), P("ctx", "head"), P("ctx"), P("head", None))
    out_specs = P("head", "ctx")
    return jax.shard_map(body, mesh=mesh, in_specs=in_specs, out_specs=out_specs, check_vma=False)
```

```python
import functools

import jax
import jax.numpy as jnp
from jax import lax
from jax.experimental import pallas as pl
from jax.experimental.pallas import tpu as pltpu
from jax.sharding import PartitionSpec as P

SCALE = 0.08838834764831845
LOG2E = 1.4426950408889634
C = SCALE * LOG2E
NEG = -1e30
HIDE = 1e30
ROWS = 512
SPAN = 256
PARTS = 4
PART = ROWS // PARTS
TILE = 256
BOTH = (2,)
OFFSETS = (4, 3, -3, 2, -2, 1, -1, 0)
f32 = jnp.float32
bf16 = jnp.bfloat16
MESH = pl.DeviceIdType.MESH


def kernel(
    q_hbm, k_hbm, v_hbm, pos_hbm, w_hbm, out_ref,
    q_ref, pos_ref, kv, posb, qT, scores, top, shift, total, acc, w_own, wT, w_oth, a_own, a_oth,
    z_out, z_in, z_out4, z_in4,
    load_sem, kv_send, kv_recv, kv_cross, pos_send, pos_recv, w_send, w_recv, w_cross,
    a_send, a_recv, z_send, z_recv,
):
    ctx = lax.axis_index("ctx")
    head = lax.axis_index("head")
    core = ctx & 1
    y = (ctx >> 1) & 3
    xh = ctx >> 3
    z = head >> 1
    xl = head & 1
    x = xh * 2 + xl

    def device(dx, dy, dz, dcore):
        nx = (x + dx) & 3
        ny = (y + dy) & 3
        nz = (z + dz) & 7
        nc = (core + dcore) & 1
        return {"ctx": ((nx >> 1) * 4 + ny) * 2 + nc, "head": nz * 2 + (nx & 1)}

    firsts = {d: device(core * d, (1 - core) * d, 0, 0) for d in (-2, -1, 1, 2)}
    second_other = {d: device((1 - core) * d, core * d, 0, 1) for d in (-1, 1)}.get
    seconds = {d: device((1 - core) * d, core * d, 0, 0) for d in (-1, 1)}
    first = firsts.get
    second = seconds.get

    other_core = device(0, 0, 0, 1)
    mate = device(1 - 2 * xl, 0, 0, 0)
    along = (device(0, 0, 1, 0), device(0, 0, -1, 0))

    def piece_of(f, s, lane):
        own = core if lane == 0 else 1 - core
        px = (x + s + own * (f - s)) & 3
        py = (y + f + own * (s - f)) & 3
        return ((px >> 1) * 4 + py) * 2 + own, px & 1

    def remote(src, dst, send_sem, recv_sem, target):
        return pltpu.make_async_remote_copy(
            src_ref=src, dst_ref=dst, send_sem=send_sem, recv_sem=recv_sem,
            device_id=target, device_id_type=MESH,
        )

    def send(src, dst, send_sem, recv_sem, target):
        remote(src, dst, send_sem, recv_sem, target).start()

    def sent_off(src, send_sem):
        remote(src, src, send_sem, load_sem.at[0], other_core).wait_send()

    def arrived(dst, recv_sem):
        remote(dst, dst, load_sem.at[0], recv_sem, other_core).wait_recv()

    loads = []

    def load(src, dst):
        copy = pltpu.make_async_copy(src, dst, load_sem.at[len(loads)])
        copy.start()
        loads.append(copy)

    my_block = ctx
    load(k_hbm, kv.at[my_block, xl, pl.ds(0, 64)])
    load(v_hbm, kv.at[my_block, xl, pl.ds(64, 64)])
    load(pos_hbm, pos_ref)
    load(q_hbm, q_ref)
    load(w_hbm, w_own)

    barrier = pltpu.get_barrier_semaphore()
    relations = [
        (h, dy, c) for h in range(2) for dy in range(4) for c in range(2) if (h, dy, c) != (0, 0, 0)
    ]
    friends = [device(2 * h, dy, 0, c) for h, dy, c in relations]
    friends += [device(1, 0, 0, 0), device(-1, 0, 0, 0), device(0, 0, 1, 0), device(0, 0, -1, 0)]
    friends += [device(1, 0, 0, 1), device(-1, 0, 0, 1)]
    for friend in friends:
        pl.semaphore_signal(barrier, inc=1, device_id=friend, device_id_type=MESH)
    for i in range(3):
        loads[i].wait()
    lane = lax.broadcasted_iota(jnp.int32, (1, 128), 1)
    posb[my_block, :, 0:128] = pos_ref[:, 0:128] - lane
    posb[my_block, :, 128:256] = pos_ref[:, SPAN : SPAN + 128] - lane
    pl.semaphore_wait(barrier, len(friends))

    passed = []

    def view_of(f, s, half):
        block, side = piece_of(f, s, 0)
        return kv.at[block, side] if half is None else kv.at[block, side, pl.ds(64 * half, 64)]

    def pass_on(f, s, target, f_there, s_there, half=None):
        view = view_of(f, s, half)
        send(view, view, kv_send.at[len(passed)],
             kv_recv.at[f_there % 4, s_there % 4, 0 if half is None else half], target)
        passed.append((f, s, half))

    def cross(f, s):
        view = view_of(f, s, None)
        send(view, view, kv_send.at[len(passed)], kv_cross.at[f, s], other_core)
        passed.append((f, s, None))

    def to_other(f, s, target, half):
        view = view_of(f, s, half)
        send(view, view, kv_send.at[len(passed)], kv_cross.at[f, 2], target)
        passed.append((f, s, half))

    def to_second(f):
        pass_on(f, 0, second(1), f, -1)
        pass_on(f, 0, second(-1), f, 1)

    def wait_piece(f, s):
        block, side = piece_of(f, s, 0)
        if s == 2 or (f, s) == (2, 0):
            for half in range(2):
                arrived(kv.at[block, side, pl.ds(64 * half, 64)], kv_recv.at[f, s, half])
        else:
            arrived(kv.at[block, side], kv_recv.at[f, s, 0])
        if s == 0:
            to_second(f)
        elif s == 3:
            pass_on(f, s, second(1), f, 2, half=0)
            if f in BOTH:
                to_other(f, s, second_other(1), half=0)
        elif s == 1:
            pass_on(f, s, second(-1), f, 2, half=1)
            if f in BOTH:
                to_other(f, s, second_other(-1), half=1)
        if s != 2 or f not in BOTH:
            cross(f, s)

    def wait_cross(f, s):
        block, side = piece_of(f, s, 1)
        arrived(kv.at[block, side], kv_cross.at[f, s])

    pass_on(0, 0, first(1), -1, 0)
    pass_on(0, 0, first(-1), 1, 0)
    pass_on(0, 0, first(2), 2, 0, half=0)
    pass_on(0, 0, first(-2), 2, 0, half=1)
    to_second(0)
    cross(0, 0)
    for i, (h, dy, c) in enumerate(relations):
        there = relations.index((h, (4 - dy) % 4, c))
        send(posb.at[my_block], posb.at[my_block], pos_send.at[i], pos_recv.at[there],
             device(2 * h, dy, 0, c))

    def weights_out(j):
        for side, d in ((0, 1), (1, -1)):
            slot = 4 * j + 2 * side + core
            offset = sum(
                (jnp.where(slot == i, o, 0) for i, o in enumerate(OFFSETS)), jnp.int32(0)
            )
            tile = ((z + offset) & 7) * 2 + 1 - xl
            send(wT.at[tile], w_oth.at[slot], w_send.at[j, side, 0], w_recv.at[j, side],
                 device(d, 0, 0, 0))

    def weights_in(j):
        for side in range(2):
            slot = 4 * j + 2 * side + core
            arrived(w_oth.at[slot], w_recv.at[j, side])
            send(w_oth.at[slot], w_oth.at[slot], w_send.at[j, side, 1], w_cross.at[j, side], other_core)

    def weights_crossed(j):
        for side in range(2):
            arrived(w_oth.at[4 * j + 2 * side + 1 - core], w_cross.at[j, side])

    loads[4].wait()
    for tile in range(16):
        wT[tile] = w_own[:, tile * 256 : (tile + 1) * 256].T
    loads[3].wait()
    for h in range(2):
        t = q_ref[:, h * 128 : (h + 1) * 128].T
        gap = jnp.zeros((64, ROWS), bf16)
        qT[h] = jnp.concatenate([t[:64], gap, t[64:], gap], axis=0)
    top[...] = jnp.full(top.shape, NEG, f32)
    total[...] = jnp.zeros(total.shape, f32)
    acc[...] = jnp.zeros(acc.shape, f32)

    row_pos = pos_ref[...]

    def starts_of(block):
        return [
            jnp.concatenate([posb[block, :, j * 128 : (j + 1) * 128]] * 4, axis=1) for j in range(2)
        ]

    def part_a(par, h, cols, k, seen, masks):
        s = jnp.dot(k, qT[h, :, cols], preferred_element_type=f32)
        if masks is not None:
            s = jnp.concatenate(
                [jnp.where(masks[j][:, cols], s[j * SPAN : (j + 1) * SPAN], NEG) for j in range(2)], axis=0
            )
        scores[par, h, :, cols] = s
        new = top[par, h, :, cols]
        for j in range(2):
            most = jnp.max(s[j * SPAN : (j + 1) * SPAN], axis=0, keepdims=True)
            new = jnp.maximum(new, jnp.where(seen[j][:, cols], most, NEG))
        top[1 - par, h, :, cols] = new
        for j in range(2):
            shift[par, h, j, :, cols] = new * C + jnp.where(seen[j][:, cols], 0.0, HIDE)

    def part_b(par, h, cols, v, fade):
        expo = [
            jnp.exp2(scores[par, h, j * SPAN : (j + 1) * SPAN, cols] * C - shift[par, h, j, :, cols])
            for j in range(2)
        ]
        total[h, :, cols] = total[h, :, cols] * fade + (
            jnp.sum(expo[0], axis=0, keepdims=True) + jnp.sum(expo[1], axis=0, keepdims=True)
        )
        more = jnp.dot(v, jnp.concatenate(expo, axis=0).astype(bf16), preferred_element_type=f32)
        acc[h, :, cols] = acc[h, :, cols] * fade + more

    tiles = [(h, slice(r * TILE, (r + 1) * TILE)) for r in range(ROWS // TILE) for h in range(2)]

    def keys_of(block):
        return jnp.concatenate([kv[block, 0], kv[block, 1]], axis=0).T

    def values_of(block):
        return jnp.concatenate([kv[block, 0, 64:], kv[block, 1, 64:]], axis=0)

    def fade_of(n, h, cols):
        par = n % 2
        return jnp.exp2((top[par, h, :, cols] - top[1 - par, h, :, cols]) * C)

    groups = (
        ((1, 0), (3, 0), (2, 0), (0, 1), (0, 3)),
        ((1, 1), (1, 3)),
        ((3, 1), (3, 3)),
        ((2, 1), (2, 3)),
        ((0, 2),),
        ((1, 2),),
        ((3, 2),),
        ((2, 2),),
    )
    orders = ((0, 1, 3, 2, 4, 5, 7, 6), (0, 4, 1, 3, 5, 7, 2, 6))

    coded = [sum(code << (3 * i) for i, code in enumerate(order)) for order in orders]

    def nth_block(n, which):
        number = core if which == 0 else 1 - core
        code = ((coded[0] + number * (coded[1] - coded[0])) >> (3 * n)) & 7
        return ((((xh + (code >> 2)) & 1) * 4) + ((y + code) & 3)) * 2 + number

    def own_group(g):
        for f, s in groups[g]:
            wait_piece(f, s)
        if g == 3:
            weights_out(0)
        if g == 5:
            weights_out(1)

    def cross_group(g):
        for f, s in (((0, 0),) if g == 0 else ()) + groups[g]:
            wait_cross(f, s)

    def a_beside_b(n, block, before, then=None):
        seen = [start <= row_pos for start in starts_of(block)]
        k, v = keys_of(block), values_of(before)
        for h, cols in tiles:
            fade = fade_of(n - 1, h, cols)
            part_a(n % 2, h, cols, k, seen, None)
            part_b((n - 1) % 2, h, cols, v, fade)
            if then is not None:
                then(h, cols)

    own_group(0)
    starts = starts_of(my_block)
    inside = lax.broadcasted_iota(jnp.int32, (SPAN, ROWS), 0)
    masks = [inside + start <= row_pos for start in starts]
    own_keys = keys_of(my_block)
    for h, cols in tiles:
        part_a(0, h, cols, own_keys, [start <= row_pos for start in starts], masks)
    for i, (h, dy, c) in enumerate(relations):
        block = (((xh + h) & 1) * 4 + ((y + dy) & 3)) * 2 + ((core + c) & 1)
        arrived(posb.at[block], pos_recv.at[i])

    def two_blocks(j, carry):
        for g in range(7):
            @pl.when(j == g)
            def comm(g=g):
                if g == 0:
                    cross_group(0)
                    own_group(1)
                else:
                    own_group(g + 1)
                    cross_group(g)
        a_beside_b(1, nth_block(j, 1), nth_block(j, 0))
        a_beside_b(2, nth_block(j + 1, 0), nth_block(j, 1))
        return carry

    lax.fori_loop(0, 7, two_blocks, 0)
    cross_group(7)
    weights_in(0)
    last_values = values_of(nth_block(7, 1))

    def finish(h, cols):
        part_b(1, h, cols, last_values, fade_of(1, h, cols))
        scale = 1.0 / total[h, :, cols]
        done = (acc[h, :, cols] * scale).astype(bf16)
        for i in range(TILE // PART):
            t = cols.start // PART + i
            a_own[t, h * 128 : (h + 1) * 128, :] = done[:, i * PART : (i + 1) * PART]
            if h == 1:
                send(a_own.at[t], a_oth.at[t], a_send.at[t], a_recv.at[t], mate)

    a_beside_b(1, nth_block(7, 1), nth_block(7, 0), finish)

    weights_crossed(0)

    def project(offset, t, rows=slice(None)):
        tile = ((z + offset) & 7) * 2 + xl
        return jnp.dot(wT[tile, rows], a_own[t], preferred_element_type=f32) + jnp.dot(
            w_oth[OFFSETS.index(offset), rows], a_oth[t], preferred_element_type=f32
        )

    def half_rows(d):
        return slice(d * 128, (d + 1) * 128)

    def send_half(d, half, t, sem):
        rows = pl.ds(half * 128, 128)
        send(z_out.at[d, 2, t, rows], z_in.at[d, 2, t, rows], z_send.at[d, sem, t], z_recv.at[d, sem, t],
             along[d])

    def up_and_down():
        return ((0, 1), (1, -1))

    def farthest(t, carry):
        arrived(a_oth.at[t], a_recv.at[t])
        part = project(4, t)
        for d, sign in up_and_down():
            z_out4[d, t] = part[half_rows(d)].astype(bf16)
            send(z_out4.at[d, t], z_in4.at[d, t], z_send.at[d, 3, t], z_recv.at[d, 3, t], along[d])
        for d, sign in up_and_down():
            z_out[d, 2, t, half_rows(1 - d), :] = project(sign * 3, t, half_rows(1 - d)).astype(bf16)
            send_half(d, 1 - d, t, 4)
        return carry

    def third(t, carry):
        for d, sign in up_and_down():
            part = project(sign * 3, t, half_rows(d))
            arrived(z_in4.at[d, t], z_recv.at[d, 3, t])
            z_out[d, 2, t, half_rows(d), :] = (part + z_in4[d, t].astype(f32)).astype(bf16)
            send_half(d, d, t, 2)
        return carry

    def nearer(k, t, carry):
        for d, sign in up_and_down():
            part = project(sign * k, t)
            if k == 2:
                arrived(z_in.at[d, 2, t, pl.ds((1 - d) * 128, 128)], z_recv.at[d, 4, t])
                arrived(z_in.at[d, 2, t, pl.ds(d * 128, 128)], z_recv.at[d, 2, t])
            else:
                arrived(z_in.at[d, k, t], z_recv.at[d, k, t])
            z_out[d, k - 1, t] = (part + z_in[d, k, t].astype(f32)).astype(bf16)
            send(z_out.at[d, k - 1, t], z_in.at[d, k - 1, t], z_send.at[d, k - 1, t],
                 z_recv.at[d, k - 1, t], along[d])
        return carry

    lax.fori_loop(0, PARTS, farthest, 0)
    weights_in(1)
    lax.fori_loop(0, PARTS, third, 0)
    weights_crossed(1)
    lax.fori_loop(0, PARTS, functools.partial(nearer, 2), 0)
    lax.fori_loop(0, PARTS, functools.partial(nearer, 1), 0)
    for t in range(PARTS):
        part = project(0, t)
        for d in range(2):
            arrived(z_in.at[d, 0, t], z_recv.at[d, 0, t])
        out_ref[:, t * PART : (t + 1) * PART] = (
            part + (z_in[0, 0, t].astype(f32) + z_in[1, 0, t].astype(f32))
        ).astype(bf16)

    for i, (f, s, half) in enumerate(passed):
        sent_off(view_of(f, s, half), kv_send.at[i])
    for i in range(len(relations)):
        sent_off(posb.at[my_block], pos_send.at[i])
    for j in range(2):
        for side in range(2):
            for leg in range(2):
                sent_off(wT.at[0], w_send.at[j, side, leg])
    for t in range(PARTS):
        sent_off(a_own.at[t], a_send.at[t])
        for d in range(2):
            sent_off(z_out4.at[d, t], z_send.at[d, 3, t])
            for k in range(2):
                sent_off(z_out.at[d, k, t], z_send.at[d, k, t])
            for sem in (2, 4):
                sent_off(z_out4.at[d, t], z_send.at[d, sem, t])


def body(queries, keys, values, positions, out_weight):
    hbm = pl.BlockSpec(memory_space=pltpu.HBM)
    dma = pltpu.SemaphoreType.DMA
    return pl.pallas_call(
        kernel,
        out_shape=jax.ShapeDtypeStruct((256, ROWS), bf16),
        in_specs=[hbm] * 5,
        out_specs=pl.BlockSpec(memory_space=pltpu.VMEM),
        scratch_shapes=[
            pltpu.VMEM((ROWS, 256), bf16),
            pltpu.VMEM((1, ROWS), jnp.int32),
            pltpu.VMEM((16, 2, 128, ROWS), bf16),
            pltpu.VMEM((16, 1, 256), jnp.int32),
            pltpu.VMEM((2, 256, ROWS), bf16),
            pltpu.VMEM((2, 2, ROWS, ROWS), f32),
            pltpu.VMEM((2, 2, 1, ROWS), f32),
            pltpu.VMEM((2, 2, 2, 1, ROWS), f32),
            pltpu.VMEM((2, 1, ROWS), f32),
            pltpu.VMEM((2, 128, ROWS), f32),
            pltpu.VMEM((256, 4096), bf16),
            pltpu.VMEM((16, 256, 256), bf16),
            pltpu.VMEM((8, 256, 256), bf16),
            pltpu.VMEM((PARTS, 256, PART), bf16),
            pltpu.VMEM((PARTS, 256, PART), bf16),
            pltpu.VMEM((2, 3, PARTS, 256, PART), bf16),
            pltpu.VMEM((2, 3, PARTS, 256, PART), bf16),
            pltpu.VMEM((2, PARTS, 128, PART), bf16),
            pltpu.VMEM((2, PARTS, 128, PART), bf16),
            dma((5,)),
            dma((36 + len(BOTH),)),
            dma((4, 4, 2)),
            dma((4, 4)),
            dma((15,)),
            dma((15,)),
            dma((2, 2, 2)),
            dma((2, 2)),
            dma((2, 2)),
            dma((PARTS,)),
            dma((PARTS,)),
            dma((2, 5, PARTS)),
            dma((2, 5, PARTS)),
        ],
        compiler_params=pltpu.CompilerParams(
            collective_id=0, has_side_effects=True, vmem_limit_bytes=56 << 20
        ),
        cost_estimate=pl.CostEstimate(flops=6_000_000_000, bytes_accessed=4_000_000, transcendentals=8_400_000),
    )(queries, keys.T, values.T, positions.reshape(1, ROWS), out_weight)


def solution(mesh):
    in_specs = (P("ctx", "head"), P("ctx", "head"), P("ctx", "head"), P("ctx"), P("head", None))
    out_specs = P("head", "ctx")
    return jax.shard_map(body, mesh=mesh, in_specs=in_specs, out_specs=out_specs, check_vma=False)
```
